256 devices in a mesh: tm: 4 (over y), row: 4 (over x), col: 16 (over z, core).
Axes of the slice: x: 4, y: 4, z: 8, core: 2. Of those that a mesh axis runs over, the one named last changes fastest.
Arguments:
- features: bfloat16 [16, 8, 160, 512], P('tm', 'row', 'col'), may hold values from -4200 to 4200, as said below
- gain_low: float32 [512], replicated, may hold values from 0.1 to 1.9
- bias_low: float32 [512], replicated, may hold values from -3 to 3
- w_up: bfloat16 [3, 3, 3, 512, 256], replicated, may hold values from -0.0546875 to 0.0546875
- b_up: float32 [256], replicated, may hold values from -3 to 3
- gain_high: float32 [256], replicated, may hold values from 0.1 to 1.9
- bias_high: float32 [256], replicated, may hold values from -3 to 3
- w_res: bfloat16 [3, 3, 3, 256, 256], replicated, may hold values from -0.078125 to 0.078125
- b_res: float32 [256], replicated, may hold values from -3 to 3
Outputs:
- decoded: bfloat16 [16, 16, 320, 256], P('tm', 'row', 'col')
The draws below stay inside these ranges and needn't reach their ends.
Inputs may be any that keep to these rules, and one draw needn't show every extreme that they name: Decoder features of order one to a few thousand.
All inputs are finite; a program needn't handle non-finite values.
Results may differ from the reference program's by a relative error of at most 0.013.
Values may be sent and summed in bfloat16 or wider, within the bound.
No kernel may reach another device: no remote copies, remote signals or barrier semaphores. Data moves between devices by JAX's collectives and lax.ppermute only.
A program may use at most 64 MiB of HBM per device.

```python
import math
import jax
import jax.numpy as jnp
from jax import lax

C_LOW = 512
C_HIGH = 256
GROUPS = 32
F_DEV = 4
NF = 16
NH = 8
NW = 160
N_TM = 4


def axis_scale(key, count):
    position = jnp.arange(count, dtype=jnp.float32) / max(count - 1, 1)
    jitter = jax.random.uniform(key, (count,), jnp.float32, 0.0, 1.0)
    return 3.0 ** (position + 0.8 * (jitter - 0.5))


def draw_features(key, part):
    key = jax.random.fold_in(key, 11)
    key_noise, key_channel, key_offset, key_rough, key_frame, key_row, key_col = jax.random.split(key, 7)
    full_shape = (NF, NH, NW, C_LOW)
    frame_scale = axis_scale(key_frame, NF)
    row_scale = axis_scale(key_row, NH)
    col_scale = axis_scale(key_col, NW)
    rising = frame_scale[:, None, None, None] * row_scale[None, :, None, None] * col_scale[None, None, :, None]
    noise_part = jnp.clip(jax.random.normal(key_noise, full_shape, jnp.float32), -4.0, 4.0)
    channel_scale = jnp.exp(jax.random.uniform(key_channel, (C_LOW,), jnp.float32, 0.0, math.log(3.0)))
    offset = jax.random.uniform(key_offset, (C_LOW,), jnp.float32, -1.0, 1.0)
    roughness = jax.random.uniform(key_rough, full_shape, jnp.float32, 0.5, 1.5)
    return (rising * channel_scale * (noise_part + offset) * roughness).astype(jnp.bfloat16)


def gaussian(key, dims, deviation, bound, kind=jnp.bfloat16):
    entries = jax.random.normal(key, dims, jnp.float32) * deviation
    return jnp.minimum(jnp.maximum(entries, -bound), bound).astype(kind)


def setup_inputs(seed: int = 0) -> dict:
    key_list = jax.random.split(jax.random.key(seed), 10)
    return {
        "features": draw_features(jax.random.fold_in(key_list[9], 71), 0),
        "gain_low": jnp.clip(1.0 + 0.18 * jax.random.normal(key_list[1], (C_LOW,), jnp.float32), 0.1, 1.9),
        "bias_low": gaussian(key_list[2], (C_LOW,), 0.5, 3.0, jnp.float32),
        "w_up": gaussian(key_list[3], (3, 3, 3, C_LOW, C_HIGH), (27 * C_LOW) ** -0.5, 0.0546875),
        "b_up": gaussian(key_list[4], (C_HIGH,), 0.5, 3.0, jnp.float32),
        "gain_high": jnp.clip(1.0 + 0.18 * jax.random.normal(key_list[5], (C_HIGH,), jnp.float32), 0.1, 1.9),
        "bias_high": gaussian(key_list[6], (C_HIGH,), 0.5, 3.0, jnp.float32),
        "w_res": gaussian(key_list[7], (3, 3, 3, C_HIGH, C_HIGH), (27 * C_HIGH) ** -0.5, 0.078125),
        "b_res": gaussian(key_list[8], (C_HIGH,), 0.5, 3.0, jnp.float32),
    }


def group_sums(field_in):
    frames, height, across, channels = field_in.shape
    grouped = field_in.reshape(frames, height, across, GROUPS, channels // GROUPS)
    return jnp.stack([lax.optimization_barrier(jnp.sum(grouped, axis=(0, 1, 2, 4))), lax.optimization_barrier(jnp.sum(grouped * grouped, axis=(0, 1, 2, 4)))])

def activate(field_in, running, cells_seen, gain, bias):
    group_mean = running[0] / cells_seen
    group_var = running[1] / cells_seen - group_mean * group_mean
    inv_std = lax.rsqrt(group_var + 1e-06)
    per_group = field_in.shape[-1] // GROUPS
    normed = (field_in - jnp.repeat(group_mean, per_group)) * jnp.repeat(inv_std, per_group) * gain + bias
    return jax.nn.silu(normed).astype(jnp.bfloat16)

def causal_conv(stacked, weight):
    result = lax.conv_general_dilated(stacked[None], weight, (1, 1, 1), ((0, 0), (1, 1), (1, 1)), dimension_numbers=('NDHWC', 'DHWIO', 'NDHWC'), preferred_element_type=jnp.float32)
    return result[0]

def reference(features, gain_low, bias_low, w_up, b_up, gain_high, bias_high, w_res, b_res):
    run_low = jnp.zeros((2, GROUPS), jnp.float32)
    run_high = jnp.zeros((2, GROUPS), jnp.float32)
    prev_low = jnp.zeros((2, NH, NW, C_LOW), jnp.bfloat16)
    prev_high = jnp.zeros((2, 2 * NH, 2 * NW, C_HIGH), jnp.bfloat16)
    decoded_parts = []
    for span_idx in range(N_TM):
        inputs_f = features[span_idx * F_DEV:(span_idx + 1) * F_DEV].astype(jnp.float32)
        run_low = run_low + group_sums(inputs_f)
        seen_low = float((span_idx + 1) * F_DEV * NH * NW * (C_LOW // GROUPS))
        first = activate(inputs_f, run_low, seen_low, gain_low, bias_low)
        stacked = jnp.concatenate([prev_low, first], axis=0)
        prev_low = first[-2:]
        upsampled = jnp.repeat(jnp.repeat(stacked, 2, axis=1), 2, axis=2)
        hidden = (causal_conv(upsampled, w_up) + b_up).astype(jnp.bfloat16)
        hidden_f = hidden.astype(jnp.float32)
        run_high = run_high + group_sums(hidden_f)
        seen_high = float((span_idx + 1) * F_DEV * 4 * NH * NW * (C_HIGH // GROUPS))
        second = activate(hidden_f, run_high, seen_high, gain_high, bias_high)
        stacked_high = jnp.concatenate([prev_high, second], axis=0)
        prev_high = second[-2:]
        decoded_parts.append((causal_conv(stacked_high, w_res) + b_res + hidden_f).astype(jnp.bfloat16))
    return jnp.concatenate(decoded_parts, axis=0)
```

```python
import functools

import jax
import jax.numpy as jnp
import numpy as np
from jax import lax
from jax.experimental import pallas as pl
from jax.experimental.pallas import tpu as pltpu
from jax.sharding import PartitionSpec as P

GROUPS = 32
LANES = 128
EVERY = ("tm", "row", "col")
HIGHEST = lax.Precision.HIGHEST
F32 = jnp.float32
BF16 = jnp.bfloat16
ROWS, SLOTS = 4, 16
CELLS = ROWS * SLOTS
VMEM_LIMIT = 62 * 1024 * 1024


def group_of(channel, channels):
    return lax.shift_right_logical(channel, int(np.log2(channels // GROUPS)))


def packed_sums(sums, squares):
    channels = sums.shape[-1]
    shape = (channels, LANES)
    member = group_of(lax.broadcasted_iota(jnp.int32, shape, 0), channels) == lax.broadcasted_iota(jnp.int32, shape, 1)
    both = jnp.concatenate([sums, squares, jnp.zeros((6, channels), F32)], axis=0)
    grouped = jnp.dot(both, member.astype(F32), precision=HIGHEST, preferred_element_type=F32)
    return grouped[0:1] + pltpu.roll(grouped, GROUPS, 1)[1:2]


def affine(parts, unit, gain, bias, span):
    channels = gain.shape[-1]
    spans = lax.axis_size("tm")
    each = parts.shape[0] // spans
    now = jnp.zeros((1, LANES), F32)
    before = jnp.zeros((1, LANES), F32)
    for s in range(spans):
        part = jnp.sum(parts[s * each : (s + 1) * each], axis=0, keepdims=True)
        now = now + jnp.where(s <= span, part, 0.0)
        before = before + jnp.where(s < span, part, 0.0)
    stacked = jnp.concatenate([now, before, jnp.zeros((6, LANES), F32)], axis=0)
    stacked = jnp.concatenate([stacked, pltpu.roll(stacked, LANES - GROUPS, 1)], axis=0)
    shape = (LANES, channels)
    member = group_of(lax.broadcasted_iota(jnp.int32, shape, 1), channels) == lax.broadcasted_iota(jnp.int32, shape, 0)
    spread = jnp.dot(stacked, member.astype(F32), precision=HIGHEST, preferred_element_type=F32)
    result = []
    for k in range(2):
        count = jnp.maximum(span + 1 - k, 1).astype(F32) * unit
        mean = spread[k : k + 1] / count
        var = spread[8 + k : 9 + k] / count - mean * mean
        scale = lax.rsqrt(var + 1e-06) * gain
        result.append((scale, bias - mean * scale))
    return result


def silu(x):
    return x / (1.0 + jnp.exp(-x))


def low_sums_kernel(x_ref, sums_ref, own_ref, to_right_ref, to_left_ref):
    frames, across, height, channels = x_ref.shape
    x = x_ref[...].astype(F32).reshape(frames * across * height, channels)
    row = packed_sums(jnp.sum(x, axis=0, keepdims=True), jnp.sum(x * x, axis=0, keepdims=True))
    sums_ref[...] = jnp.broadcast_to(row, sums_ref.shape)
    block = height * frames * SLOTS
    shape = (block + 32, x.shape[0])
    to = lax.broadcasted_iota(jnp.int32, shape, 0)
    edge = to - block
    k = jnp.where(to < block, to // SLOTS, edge % 16)
    column = jnp.where(to < block, to % SLOTS - 1, jnp.where(edge < 16, across - 1, 0))
    source = ((k % frames) * across + column) * height + k // frames
    hit = (lax.broadcasted_iota(jnp.int32, shape, 1) == source) & (column >= 0) & (column < across) & (k < height * frames)
    moved = jnp.dot(hit.astype(BF16), x.astype(BF16), preferred_element_type=F32).astype(BF16)
    own_ref[...] = moved[:block]
    to_right_ref[...] = moved[block : block + 16]
    to_left_ref[...] = moved[block + 16 :]


def pack_kernel(own_ref, left_ref, right_ref, out_ref):
    rows = own_ref.shape[0]
    shape = (rows, 32)
    to = lax.broadcasted_iota(jnp.int32, shape, 0)
    source = lax.broadcasted_iota(jnp.int32, shape, 1)
    slot, k = to % SLOTS, to // SLOTS
    hit = ((slot == 0) & (source == k)) | ((slot == 11) & (source == 16 + k))
    both = jnp.concatenate([left_ref[...], right_ref[...]], axis=0)
    moved = jnp.dot(hit.astype(BF16), both, preferred_element_type=F32)
    out_ref[...] = (own_ref[...].astype(F32) + moved).astype(BF16)


def position():
    tm, row, col = (lax.axis_index(a) for a in EVERY)
    return tm, row, col


def up_kernel(spans_used, unit, parts_ref, gain_ref, bias_ref, b_ref, *refs):
    n_prev, n_now = spans_used
    own = n_now > 0
    if own:
        now_ref, prev_ref, above_ref, below_ref, w_ref, hid_ref, sums_ref, x_ref, wbuf, sems = refs
    else:
        prev_ref, above_ref, below_ref, w_ref, _, hid_ref, x_ref, wbuf, sems = refs
    copies = [pltpu.make_async_copy(w_ref.at[:, k // 3, k % 3], wbuf.at[k], sems.at[k]) for k in range(9)]
    for copy in copies:
        copy.start()
    tm, row, col = position()
    last_row, last_col = lax.axis_size("row") - 1, lax.axis_size("col") - 1
    (scale, offset), (scale_prev, offset_prev) = affine(parts_ref[...], unit, gain_ref[...], bias_ref[...], tm)
    depth = scale.shape[-1]
    line = prev_ref.shape[0] // 2
    span = line // SLOTS
    slot = lax.broadcasted_iota(jnp.int32, (line, depth), 0) % SLOTS
    inside = (slot >= jnp.where(col > 0, 0, 1)) & (slot <= jnp.where(col < last_col, 11, 10))

    def place(piece, first, count, at, r, a, b, valid):
        v = silu(piece[first * SLOTS : (first + count) * SLOTS].astype(F32) * a + b)
        v = jnp.where(inside[: count * SLOTS] & valid, v, 0.0).astype(BF16)
        for f in range(count):
            x_ref[at + f, r * SLOTS : (r + 1) * SLOTS] = v[f * SLOTS : (f + 1) * SLOTS]

    past = tm > 0
    up, down = row > 0, row < last_row
    first = span - n_prev
    for r in range(2):
        place(prev_ref.at[r * line : (r + 1) * line], first, n_prev, 0, r + 1, scale_prev, offset_prev, past)
    place(above_ref.at[line:], first, n_prev, 0, 0, scale_prev, offset_prev, past & up)
    place(below_ref.at[line:], first, n_prev, 0, 3, scale_prev, offset_prev, past & down)
    if own:
        for r in range(2):
            place(now_ref.at[r * line : (r + 1) * line], 0, n_now, n_prev, r + 1, scale, offset, tm >= 0)
        place(above_ref.at[:line], 0, n_now, n_prev, 0, scale, offset, up)
        place(below_ref.at[:line], 0, n_now, n_prev, 3, scale, offset, down)

    frames = n_prev + n_now - 2
    size = frames * CELLS
    width = b_ref.shape[-1]
    x = jnp.concatenate([x_ref[a : a + frames].reshape(size, depth) for a in range(3)], axis=1)
    acc = [[None, None], [None, None]]

    def add(p, q, value):
        acc[p][q] = value if acc[p][q] is None else acc[p][q] + value

    for b in range(3):
        z = []
        for e in range(3):
            copies[3 * b + e].wait()
            z.append(jnp.dot(x, wbuf[3 * b + e].reshape(3 * depth, width), preferred_element_type=F32))
        even = pltpu.roll(z[0], 1, 0) + (z[1] + z[2])
        odd = (z[0] + z[1]) + pltpu.roll(z[2], size - 1, 0)
        for q, u in ((0, even), (1, odd)):
            add(0, q, pltpu.roll(u, SLOTS, 0) if b == 0 else u)
            add(1, q, pltpu.roll(u, size - SLOTS, 0) if b == 2 else u)
    total = jnp.zeros((1, width), F32)
    square = jnp.zeros((1, width), F32)
    if own:
        at = lax.broadcasted_iota(jnp.int32, (frames, 2, SLOTS, width), 2)
        mine = (at >= 1) & (at <= 10)
    for p in range(2):
        for q in range(2):
            hidden = (acc[p][q] + b_ref[...]).astype(BF16)
            for f in range(frames):
                hid_ref[f, (2 * p + q) * CELLS : (2 * p + q + 1) * CELLS] = hidden[f * CELLS : (f + 1) * CELLS]
            if own:
                seen = hidden.astype(F32).reshape(frames, ROWS, SLOTS, width)[:, 1:3]
                seen = jnp.where(mine, seen, 0.0).reshape(-1, width)
                total = total + jnp.sum(seen, axis=0, keepdims=True)
                square = square + jnp.sum(seen * seen, axis=0, keepdims=True)
    if own:
        sums_ref[...] = jnp.broadcast_to(packed_sums(total, square), sums_ref.shape)


def gather_matrix():
    m = np.zeros((3, 3, 20, 4, 2, 2, ROWS, SLOTS), np.float32)
    for b in range(3):
        for e in range(3):
            for y in range(4):
                for x in range(20):
                    v, u = y + b - 1, x + e - 1
                    m[b, e, x, y, v % 2, u % 2, v // 2 + 1, u // 2 + 1] = 1.0
    return m.reshape(720, 4 * CELLS)


def res_kernel(unit, parts_ref, gain_ref, bias_ref, b_ref, hid_ref, hid_prev_ref, pick_ref, w_ref, out_ref, g_ref, wbuf, sems):
    copies = [pltpu.make_async_copy(w_ref.at[k], wbuf.at[k], sems.at[k]) for k in range(3)]
    for copy in copies:
        copy.start()
    tm, row, col = position()
    last_row, last_col = lax.axis_size("row") - 1, lax.axis_size("col") - 1
    (scale, offset), (scale_prev, offset_prev) = affine(parts_ref[...], unit, gain_ref[...], bias_ref[...], tm)
    width = scale.shape[-1]
    cell = lax.broadcasted_iota(jnp.int32, (4 * CELLS, width), 0)
    parity, r, slot = cell // CELLS, (cell // SLOTS) % ROWS, cell % SLOTS
    y, x = 2 * (r - 1) + parity // 2, 2 * (slot - 1) + parity % 2
    inside = ((y >= 0) | (row > 0)) & ((y < 4) | (row < last_row)) & ((x >= 0) | (col > 0)) & ((x < 20) | (col < last_col))
    n_prev, n_now = hid_prev_ref.shape[0], hid_ref.shape[0]
    area = 80
    for f in range(n_prev + n_now):
        if f < n_prev:
            v = silu(hid_prev_ref[f].astype(F32) * scale_prev + offset_prev)
            v = jnp.where(inside & (tm > 0), v, 0.0)
        else:
            v = silu(hid_ref[f - n_prev].astype(F32) * scale + offset)
            v = jnp.where(inside, v, 0.0)
        picked = jnp.dot(pick_ref[...], v.astype(BF16), preferred_element_type=F32).astype(BF16)
        for k in range(9):
            g_ref[f * area : (f + 1) * area, k * width : (k + 1) * width] = picked[k * area : (k + 1) * area]
    total = None
    for a in range(3):
        copies[a].wait()
        part = jnp.dot(
            g_ref[a * area : (a + n_now) * area], wbuf[a].reshape(9 * width, width), preferred_element_type=F32
        )
        total = part if total is None else total + part
    for f in range(n_now):
        hidden = jnp.dot(pick_ref[4 * area : 5 * area], hid_ref[f], preferred_element_type=F32)
        decoded = total[f * area : (f + 1) * area] + b_ref[...] + hidden
        out_ref[f] = decoded.reshape(out_ref.shape[1:]).astype(BF16)


def shifted(value, axes, sizes, steps):
    place = np.arange(int(np.prod(sizes))).reshape(sizes)
    route = []
    for at in np.ndindex(*sizes):
        to = tuple(i + s for i, s in zip(at, steps))
        if all(0 <= t < n for t, n in zip(to, sizes)):
            route.append((int(place[at]), int(place[to])))
    return lax.ppermute(value, axes, route)


def params(**kw):
    return pltpu.CompilerParams(vmem_limit_bytes=VMEM_LIMIT, **kw)


VM = pl.BlockSpec(memory_space=pltpu.VMEM)
HBM = pl.BlockSpec(memory_space=pltpu.HBM)


def local(features, gain_low, bias_low, w_up, b_up, gain_high, bias_high, w_res, b_res):
    n_tm, n_row, n_col = (lax.axis_size(a) for a in EVERY)
    devices = n_tm * n_row * n_col
    frames, height, across, depth = features.shape
    width = w_up.shape[-1]
    low_unit = float(n_row * n_col * frames * height * across * (depth // GROUPS))
    high_unit = float(n_row * n_col * frames * 4 * height * across * (width // GROUPS))

    block = height * frames * SLOTS
    line = frames * SLOTS
    sums, own, to_right, to_left = pl.pallas_call(
        low_sums_kernel,
        out_shape=(
            jax.ShapeDtypeStruct((devices, LANES), F32),
            jax.ShapeDtypeStruct((block, depth), BF16),
            jax.ShapeDtypeStruct((16, depth), BF16),
            jax.ShapeDtypeStruct((16, depth), BF16),
        ),
        in_specs=[VM],
        out_specs=(VM,) * 4,
        compiler_params=params(),
        name="low_sums",
    )(features.transpose(0, 2, 1, 3))
    left = shifted(to_right, "col", (n_col,), (1,))
    right = shifted(to_left, "col", (n_col,), (-1,))
    low_parts = lax.all_to_all(sums, EVERY, 0, 0)
    now = pl.pallas_call(
        pack_kernel,
        out_shape=jax.ShapeDtypeStruct((block, depth), BF16),
        in_specs=[VM] * 3,
        out_specs=VM,
        compiler_params=params(),
        name="pack",
    )(own, left, right)
    prev = shifted(now, "tm", (n_tm,), (1,))
    above = shifted(jnp.concatenate([now[line:], prev[line:]], axis=0), "row", (n_row,), (1,))
    below = shifted(jnp.concatenate([now[:line], prev[:line]], axis=0), "row", (n_row,), (-1,))

    gl, bl, bu = gain_low.reshape(1, -1), bias_low.reshape(1, -1), b_up.reshape(1, -1)
    gh, bh, br = gain_high.reshape(1, -1), bias_high.reshape(1, -1), b_res.reshape(1, -1)

    def scratch(count):
        return [
            pltpu.VMEM((count, CELLS, depth), BF16),
            pltpu.VMEM((9, 3, depth, width), BF16),
            pltpu.SemaphoreType.DMA((9,)),
        ]

    hidden, high_sums = pl.pallas_call(
        functools.partial(up_kernel, (2, frames), low_unit),
        out_shape=(
            jax.ShapeDtypeStruct((frames, 4 * CELLS, width), BF16),
            jax.ShapeDtypeStruct((devices, LANES), F32),
        ),
        in_specs=[VM] * 8 + [HBM],
        out_specs=(VM, VM),
        scratch_shapes=scratch(2 + frames),
        compiler_params=params(),
        name="up_now",
    )(low_parts, gl, bl, bu, now, prev, above, below, w_up)
    high_parts = lax.all_to_all(high_sums, EVERY, 0, 0)
    hidden_prev = pl.pallas_call(
        functools.partial(up_kernel, (frames, 0), low_unit),
        out_shape=jax.ShapeDtypeStruct((2, 4 * CELLS, width), BF16),
        in_specs=[VM] * 7 + [HBM, HBM],
        out_specs=VM,
        scratch_shapes=scratch(frames),
        compiler_params=params(),
        cost_estimate=pl.CostEstimate(flops=27 * 2 * 128 * 512 * 256, bytes_accessed=27 * 512 * 256 * 2, transcendentals=0),
        name="up_prev",
    )(low_parts, gl, bl, bu, prev, above, below, w_up, hidden)

    area = 4 * height * across
    decoded = pl.pallas_call(
        functools.partial(res_kernel, high_unit),
        out_shape=jax.ShapeDtypeStruct((frames, 2 * across, 2 * height, width), BF16),
        in_specs=[VM] * 7 + [HBM],
        out_specs=VM,
        scratch_shapes=[
            pltpu.VMEM(((2 + frames) * area, 9 * width), BF16),
            pltpu.VMEM((3, 3, 3, width, width), BF16),
            pltpu.SemaphoreType.DMA((3,)),
        ],
        compiler_params=params(),
        name="res",
    )(high_parts, gh, bh, br, hidden, hidden_prev, jnp.asarray(gather_matrix(), BF16), w_res)
    return decoded.transpose(0, 2, 1, 3)


def solution(mesh):
    in_specs = (P("tm", "row", "col", None), P(), P(), P(), P(), P(), P(), P(), P())
    out_specs = P("tm", "row", "col", None)
    return jax.shard_map(local, mesh=mesh, in_specs=in_specs, out_specs=out_specs, check_vma=False)
```

```python
import functools

import jax
import jax.numpy as jnp
import numpy as np
from jax import lax
from jax.experimental import pallas as pl
from jax.experimental.pallas import tpu as pltpu
from jax.sharding import PartitionSpec as P

GROUPS = 32
LANES = 128
EVERY = ("tm", "row", "col")
HIGHEST = lax.Precision.HIGHEST
F32 = jnp.float32
BF16 = jnp.bfloat16
ROWS, SLOTS = 4, 16
CELLS = ROWS * SLOTS
MIB = 1024 * 1024


def group_of(channel, channels):
    return lax.shift_right_logical(channel, int(np.log2(channels // GROUPS)))


def packed_sums(sums, squares):
    channels = sums.shape[-1]
    shape = (channels, LANES)
    member = group_of(lax.broadcasted_iota(jnp.int32, shape, 0), channels) == lax.broadcasted_iota(jnp.int32, shape, 1)
    both = jnp.concatenate([sums, squares, jnp.zeros((6, channels), F32)], axis=0)
    grouped = jnp.dot(both, member.astype(F32), precision=HIGHEST, preferred_element_type=F32)
    return grouped[0:1] + pltpu.roll(grouped, GROUPS, 1)[1:2]


def affine(parts, unit, gain, bias, span):
    channels = gain.shape[-1]
    spans = lax.axis_size("tm")
    each = parts.shape[0] // spans
    now = jnp.zeros((1, LANES), F32)
    before = jnp.zeros((1, LANES), F32)
    for s in range(spans):
        part = jnp.sum(parts[s * each : (s + 1) * each], axis=0, keepdims=True)
        now = now + jnp.where(s <= span, part, 0.0)
        before = before + jnp.where(s < span, part, 0.0)
    stacked = jnp.concatenate([now, before, jnp.zeros((6, LANES), F32)], axis=0)
    stacked = jnp.concatenate([stacked, pltpu.roll(stacked, LANES - GROUPS, 1)], axis=0)
    shape = (LANES, channels)
    member = group_of(lax.broadcasted_iota(jnp.int32, shape, 1), channels) == lax.broadcasted_iota(jnp.int32, shape, 0)
    spread = jnp.dot(stacked, member.astype(F32), precision=HIGHEST, preferred_element_type=F32)
    result = []
    for k in range(2):
        count = jnp.maximum(span + 1 - k, 1).astype(F32) * unit
        mean = spread[k : k + 1] / count
        var = spread[8 + k : 9 + k] / count - mean * mean
        scale = lax.rsqrt(var + 1e-06) * gain
        result.append((scale, bias - mean * scale))
    return result


def silu(x):
    return x / (1.0 + jnp.exp(-x))


def low_sums_kernel(x_ref, sums_ref, own_ref, to_right_ref, to_left_ref):
    frames, across, height, channels = x_ref.shape
    x = x_ref[...].astype(F32).reshape(frames * across * height, channels)
    row = packed_sums(jnp.sum(x, axis=0, keepdims=True), jnp.sum(x * x, axis=0, keepdims=True))
    sums_ref[...] = jnp.broadcast_to(row, sums_ref.shape)
    block = height * frames * SLOTS
    shape = (block + 32, x.shape[0])
    to = lax.broadcasted_iota(jnp.int32, shape, 0)
    edge = to - block
    k = jnp.where(to < block, to // SLOTS, edge % 16)
    column = jnp.where(to < block, to % SLOTS - 1, jnp.where(edge < 16, across - 1, 0))
    source = ((k % frames) * across + column) * height + k // frames
    hit = (lax.broadcasted_iota(jnp.int32, shape, 1) == source) & (column >= 0) & (column < across) & (k < height * frames)
    moved = jnp.dot(hit.astype(BF16), x.astype(BF16), preferred_element_type=F32).astype(BF16)
    own_ref[...] = moved[:block]
    to_right_ref[...] = moved[block : block + 16]
    to_left_ref[...] = moved[block + 16 :]


def pack_kernel(own_ref, left_ref, right_ref, prev_own_ref, prev_left_ref, prev_right_ref, gain_ref, bias_ref, b_ref, now_ref, prev_ref, up_ref, down_ref, par_ref):
    rows = own_ref.shape[0]
    line = rows // 2
    shape = (rows, 32)
    to = lax.broadcasted_iota(jnp.int32, shape, 0)
    source = lax.broadcasted_iota(jnp.int32, shape, 1)
    slot, k = to % SLOTS, to // SLOTS
    hit = (((slot == 0) & (source == k)) | ((slot == 11) & (source == 16 + k))).astype(BF16)
    for j, (own, left, right, out) in enumerate(
        ((own_ref, left_ref, right_ref, now_ref), (prev_own_ref, prev_left_ref, prev_right_ref, prev_ref))
    ):
        both = jnp.concatenate([left[...], right[...]], axis=0)
        moved = jnp.dot(hit, both, preferred_element_type=F32)
        block = (own[...].astype(F32) + moved).astype(BF16)
        out[...] = block
        up_ref[j * line : (j + 1) * line] = block[:line]
        down_ref[j * line : (j + 1) * line] = block[line:]
    par_ref[0:1] = gain_ref[...]
    par_ref[1:2] = bias_ref[...]
    par_ref[2:3, : b_ref.shape[1]] = b_ref[...]


def position():
    tm, row, col = (lax.axis_index(a) for a in EVERY)
    return tm, row, col


def up_kernel(
    unit,
    parts_ref,
    par_ref,
    now_ref,
    prev_ref,
    above_ref,
    below_ref,
    w_ref,
    hid_ref,
    sums_ref,
    x_ref,
    wbuf,
    sems,
):
    copies = [pltpu.make_async_copy(w_ref.at[:, k // 3, k % 3], wbuf.at[k], sems.at[k]) for k in range(9)]
    for copy in copies:
        copy.start()
    tm, row, col = position()
    last_row, last_col = lax.axis_size("row") - 1, lax.axis_size("col") - 1
    (scale, offset), (scale_prev, offset_prev) = affine(parts_ref[...], unit, par_ref[0:1], par_ref[1:2], tm)
    depth = scale.shape[-1]
    line = prev_ref.shape[0] // 2
    span = line // SLOTS
    slot = lax.broadcasted_iota(jnp.int32, (line, depth), 0) % SLOTS
    inside = (slot >= jnp.where(col > 0, 0, 1)) & (slot <= jnp.where(col < last_col, 11, 10))

    def place(piece, at, r, a, b, valid):
        v = silu(piece[...].astype(F32) * a + b)
        v = jnp.where(inside & valid, v, 0.0).astype(BF16)
        for f in range(span):
            x_ref[at + f, r * SLOTS : (r + 1) * SLOTS] = v[f * SLOTS : (f + 1) * SLOTS]

    past = tm > 0
    up, down = row > 0, row < last_row
    for r in range(2):
        half = slice(r * line, (r + 1) * line)
        place(prev_ref.at[half], 0, r + 1, scale_prev, offset_prev, past)
        place(now_ref.at[half], span, r + 1, scale, offset, tm >= 0)
    for r, ref, valid in ((0, above_ref, up), (3, below_ref, down)):
        place(ref.at[line:], 0, r, scale_prev, offset_prev, past & valid)
        place(ref.at[:line], span, r, scale, offset, valid)

    frames = 2 * span - 2
    size = frames * CELLS
    width = wbuf.shape[-1]
    up_bias = par_ref[2:3, :width]
    x = jnp.concatenate([x_ref[a : a + frames].reshape(size, depth) for a in range(3)], axis=1)
    acc = [[None, None], [None, None]]

    def add(p, q, value):
        acc[p][q] = value if acc[p][q] is None else acc[p][q] + value

    for b in range(3):
        z = []
        for e in range(3):
            copies[3 * b + e].wait()
            z.append(jnp.dot(x, wbuf[3 * b + e].reshape(3 * depth, width), preferred_element_type=F32))
        even = pltpu.roll(z[0], 1, 0) + (z[1] + z[2])
        odd = (z[0] + z[1]) + pltpu.roll(z[2], size - 1, 0)
        for q, u in ((0, even), (1, odd)):
            add(0, q, pltpu.roll(u, SLOTS, 0) if b == 0 else u)
            add(1, q, pltpu.roll(u, size - SLOTS, 0) if b == 2 else u)
    total = jnp.zeros((1, width), F32)
    square = jnp.zeros((1, width), F32)
    at = lax.broadcasted_iota(jnp.int32, (span, 2, SLOTS, width), 2)
    mine = (at >= 1) & (at <= 10)
    for p in range(2):
        for q in range(2):
            hidden = (acc[p][q] + up_bias).astype(BF16)
            for f in range(frames):
                hid_ref[f, (2 * p + q) * CELLS : (2 * p + q + 1) * CELLS] = hidden[f * CELLS : (f + 1) * CELLS]
            seen = hidden[frames * CELLS - span * CELLS :].astype(F32).reshape(span, ROWS, SLOTS, width)[:, 1:3]
            seen = jnp.where(mine, seen, 0.0).reshape(-1, width)
            total = total + jnp.sum(seen, axis=0, keepdims=True)
            square = square + jnp.sum(seen * seen, axis=0, keepdims=True)
    sums_ref[...] = jnp.broadcast_to(packed_sums(total, square), sums_ref.shape)


def gather_matrix():
    m = np.zeros((3, 3, 20, 4, 2, 2, ROWS, SLOTS), np.float32)
    for b in range(3):
        for e in range(3):
            for y in range(4):
                for x in range(20):
                    v, u = y + b - 1, x + e - 1
                    m[b, e, x, y, v % 2, u % 2, v // 2 + 1, u // 2 + 1] = 1.0
    return m.reshape(720, 4 * CELLS)


def res_kernel(unit, parts_ref, gain_ref, bias_ref, b_ref, hid_ref, pick_ref, w_ref, out_ref, g_ref, wbuf, sems):
    copies = [pltpu.make_async_copy(w_ref.at[k], wbuf.at[k], sems.at[k]) for k in range(3)]
    for copy in copies:
        copy.start()
    tm, row, col = position()
    last_row, last_col = lax.axis_size("row") - 1, lax.axis_size("col") - 1
    (scale, offset), (scale_prev, offset_prev) = affine(parts_ref[...], unit, gain_ref[...], bias_ref[...], tm)
    width = scale.shape[-1]
    cell = lax.broadcasted_iota(jnp.int32, (4 * CELLS, width), 0)
    parity, r, slot = cell // CELLS, (cell // SLOTS) % ROWS, cell % SLOTS
    y, x = 2 * (r - 1) + parity // 2, 2 * (slot - 1) + parity % 2
    inside = ((y >= 0) | (row > 0)) & ((y < 4) | (row < last_row)) & ((x >= 0) | (col > 0)) & ((x < 20) | (col < last_col))
    n_now = out_ref.shape[0]
    n_prev = hid_ref.shape[0] - n_now
    area = 80
    for f in range(n_prev + n_now):
        a, b = (scale_prev, offset_prev) if f < n_prev else (scale, offset)
        valid = inside & (tm > 0) if f < n_prev else inside
        v = jnp.where(valid, silu(hid_ref[f].astype(F32) * a + b), 0.0)
        picked = jnp.dot(pick_ref[...], v.astype(BF16), preferred_element_type=F32).astype(BF16)
        for k in range(9):
            g_ref[f * area : (f + 1) * area, k * width : (k + 1) * width] = picked[k * area : (k + 1) * area]
    total = None
    for a in range(3):
        copies[a].wait()
        part = jnp.dot(
            g_ref[a * area : (a + n_now) * area], wbuf[a].reshape(9 * width, width), preferred_element_type=F32
        )
        total = part if total is None else total + part
    for f in range(n_now):
        hidden = jnp.dot(pick_ref[4 * area : 5 * area], hid_ref[n_prev + f], preferred_element_type=F32)
        decoded = total[f * area : (f + 1) * area] + b_ref[...] + hidden
        out_ref[f] = decoded.reshape(out_ref.shape[1:]).astype(BF16)


def shifted(value, axes, steps):
    sizes = tuple(lax.axis_size(a) for a in axes)
    place = np.arange(int(np.prod(sizes))).reshape(sizes)
    route = [(int(place[at]), int(place[tuple((i + s) % n for i, s, n in zip(at, steps, sizes))])) for at in np.ndindex(*sizes)]
    return lax.ppermute(value, axes, route)


def params(mib):
    return pltpu.CompilerParams(vmem_limit_bytes=mib * MIB)


def in_hbm(array):
    return pltpu.with_memory_space_constraint(array, pltpu.HBM)


VM = pl.BlockSpec(memory_space=pltpu.VMEM)
HBM = pl.BlockSpec(memory_space=pltpu.HBM)


def local(features, gain_low, bias_low, w_up, b_up, gain_high, bias_high, w_res, b_res):
    n_tm, n_row, n_col = (lax.axis_size(a) for a in EVERY)
    devices = n_tm * n_row * n_col
    frames, height, across, depth = features.shape
    width = w_up.shape[-1]
    low_unit = float(n_row * n_col * frames * height * across * (depth // GROUPS))
    high_unit = float(n_row * n_col * frames * 4 * height * across * (width // GROUPS))

    block = height * frames * SLOTS
    line = frames * SLOTS
    sums, own, to_right, to_left = pl.pallas_call(
        low_sums_kernel,
        out_shape=(
            jax.ShapeDtypeStruct((devices, LANES), F32),
            jax.ShapeDtypeStruct((block, depth), BF16),
            jax.ShapeDtypeStruct((16, depth), BF16),
            jax.ShapeDtypeStruct((16, depth), BF16),
        ),
        in_specs=[VM],
        out_specs=(VM,) * 4,
        compiler_params=params(16),
        name="low_sums",
    )(features.transpose(0, 2, 1, 3))
    prev_own = shifted(own, ("tm",), (1,))
    prev_left = shifted(to_right, ("tm", "col"), (1, 1))
    prev_right = shifted(to_left, ("tm", "col"), (1, -1))
    left = shifted(to_right, ("col",), (1,))
    right = shifted(to_left, ("col",), (-1,))
    low_parts = lax.all_to_all(sums, EVERY, 0, 0)
    gl, bl, bu = gain_low.reshape(1, -1), bias_low.reshape(1, -1), b_up.reshape(1, -1)
    gh, bh, br = gain_high.reshape(1, -1), bias_high.reshape(1, -1), b_res.reshape(1, -1)
    now, prev, up, down, par = pl.pallas_call(
        pack_kernel,
        out_shape=(jax.ShapeDtypeStruct((block, depth), BF16),) * 4 + (jax.ShapeDtypeStruct((8, depth), F32),),
        in_specs=[VM] * 9,
        out_specs=(VM,) * 5,
        compiler_params=params(16),
        name="pack",
    )(own, left, right, prev_own, prev_left, prev_right, in_hbm(gl), in_hbm(bl), in_hbm(bu))
    above = shifted(down, ("row",), (1,))
    below = shifted(up, ("row",), (-1,))

    hidden, high_sums = pl.pallas_call(
        functools.partial(up_kernel, low_unit),
        out_shape=(
            jax.ShapeDtypeStruct((2 + frames, 4 * CELLS, width), BF16),
            jax.ShapeDtypeStruct((devices, LANES), F32),
        ),
        in_specs=[VM] * 6 + [HBM],
        out_specs=(VM, VM),
        scratch_shapes=[
            pltpu.VMEM((2 * frames, CELLS, depth), BF16),
            pltpu.VMEM((9, 3, depth, width), BF16),
            pltpu.SemaphoreType.DMA((9,)),
        ],
        compiler_params=params(28),
        name="up",
    )(low_parts, par, now, prev, above, below, in_hbm(w_up))
    high_parts = lax.all_to_all(high_sums, EVERY, 0, 0)

    area = 4 * height * across
    decoded = pl.pallas_call(
        functools.partial(res_kernel, high_unit),
        out_shape=jax.ShapeDtypeStruct((frames, 2 * across, 2 * height, width), BF16),
        in_specs=[VM] * 6 + [HBM],
        out_specs=VM,
        scratch_shapes=[
            pltpu.VMEM(((2 + frames) * area, 9 * width), BF16),
            pltpu.VMEM((3, 3, 3, width, width), BF16),
            pltpu.SemaphoreType.DMA((3,)),
        ],
        compiler_params=params(24),
        name="res",
    )(high_parts, gh, bh, br, hidden, jnp.asarray(gather_matrix(), BF16), in_hbm(w_res))
    return decoded.transpose(0, 2, 1, 3)


def solution(mesh):
    in_specs = (P("tm", "row", "col", None), P(), P(), P(), P(), P(), P(), P(), P())
    out_specs = P("tm", "row", "col", None)
    return jax.shard_map(local, mesh=mesh, in_specs=in_specs, out_specs=out_specs, check_vma=False)
```

```python
import functools

import jax
import jax.numpy as jnp
import numpy as np
from jax import lax
from jax.experimental import pallas as pl
from jax.experimental.pallas import tpu as pltpu
from jax.sharding import PartitionSpec as P

GROUPS = 32
LANES = 128
EVERY = ("tm", "row", "col")
HIGHEST = lax.Precision.HIGHEST
F32 = jnp.float32
BF16 = jnp.bfloat16
ROWS, ACROSS, SLOTS = 4, 12, 16
CELLS = ROWS * ACROSS
MIB = 1024 * 1024


def group_of(channel, channels):
    return lax.shift_right_logical(channel, int(np.log2(channels // GROUPS)))


def packed_sums(sums, squares):
    channels = sums.shape[-1]
    shape = (channels, LANES)
    member = group_of(lax.broadcasted_iota(jnp.int32, shape, 0), channels) == lax.broadcasted_iota(jnp.int32, shape, 1)
    both = jnp.concatenate([sums, squares, jnp.zeros((6, channels), F32)], axis=0)
    grouped = jnp.dot(both, member.astype(F32), precision=HIGHEST, preferred_element_type=F32)
    return grouped[0:1] + pltpu.roll(grouped, GROUPS, 1)[1:2]


def affine(parts, unit, gain, bias, span):
    channels = gain.shape[-1]
    spans = lax.axis_size("tm")
    each = parts.shape[0] // spans
    now = jnp.zeros((1, LANES), F32)
    before = jnp.zeros((1, LANES), F32)
    for s in range(spans):
        part = jnp.sum(parts[s * each : (s + 1) * each], axis=0, keepdims=True)
        now = now + jnp.where(s <= span, part, 0.0)
        before = before + jnp.where(s < span, part, 0.0)
    stacked = jnp.concatenate([now, before, jnp.zeros((6, LANES), F32)], axis=0)
    stacked = jnp.concatenate([stacked, pltpu.roll(stacked, LANES - GROUPS, 1)], axis=0)
    shape = (LANES, channels)
    member = group_of(lax.broadcasted_iota(jnp.int32, shape, 1), channels) == lax.broadcasted_iota(jnp.int32, shape, 0)
    spread = jnp.dot(stacked, member.astype(F32), precision=HIGHEST, preferred_element_type=F32)
    result = []
    for k in range(2):
        count = jnp.maximum(span + 1 - k, 1).astype(F32) * unit
        mean = spread[k : k + 1] / count
        var = spread[8 + k : 9 + k] / count - mean * mean
        scale = lax.rsqrt(var + 1e-06) * gain
        result.append((scale, bias - mean * scale))
    return result


def silu(x):
    return x / (1.0 + jnp.exp(-x))


def low_sums_kernel(x_ref, sums_ref):
    x = x_ref[...].astype(F32)
    row = packed_sums(jnp.sum(x, axis=0, keepdims=True), jnp.sum(x * x, axis=0, keepdims=True))
    sums_ref[...] = jnp.broadcast_to(row, sums_ref.shape)


def lay_out_kernel(x_ref, own_ref, to_core_ref, to_chip_ref):
    frames, across, height, channels = x_ref.shape
    x = x_ref[...].astype(F32).reshape(frames * across * height, channels)
    block = height * frames * SLOTS
    shape = (block + 32, x.shape[0])
    to = lax.broadcasted_iota(jnp.int32, shape, 0)
    edge = to - block
    odd = lax.axis_index("col") % 2
    last = (edge < 16).astype(jnp.int32) != odd
    k = jnp.where(to < block, to // SLOTS, edge % 16)
    column = jnp.where(to < block, to % SLOTS - 1, jnp.where(last, across - 1, 0))
    source = ((k % frames) * across + column) * height + k // frames
    hit = (lax.broadcasted_iota(jnp.int32, shape, 1) == source) & (column >= 0) & (column < across) & (k < height * frames)
    moved = jnp.dot(hit.astype(BF16), x.astype(BF16), preferred_element_type=F32).astype(BF16)
    own_ref[...] = moved[:block]
    to_core_ref[...] = moved[block : block + 16]
    to_chip_ref[...] = moved[block + 16 :]


def narrow(rows):
    shape = (rows // 16 * 12, rows)
    to, source = (lax.broadcasted_iota(jnp.int32, shape, d) for d in range(2))
    return (source == to // 12 * SLOTS + to % 12).astype(BF16)


def widen(rows):
    shape = (rows // 12 * 16, rows)
    to, source = (lax.broadcasted_iota(jnp.int32, shape, d) for d in range(2))
    return ((to % SLOTS < 12) & (source == to // SLOTS * 12 + to % SLOTS)).astype(BF16)


def pack_kernel(own_ref, core_ref, chip_ref, prev_own_ref, prev_core_ref, prev_chip_ref, now_ref, prev_ref, up_ref, down_ref):
    rows = own_ref.shape[0]
    line = rows // 2
    shape = (rows, 32)
    to = lax.broadcasted_iota(jnp.int32, shape, 0)
    source = lax.broadcasted_iota(jnp.int32, shape, 1)
    core_slot = jnp.where(lax.axis_index("col") % 2 == 0, 11, 0)
    slot, k = to % SLOTS, to // SLOTS
    hit = (((slot == core_slot) & (source == k)) | ((slot == 11 - core_slot) & (source == 16 + k))).astype(BF16)
    take = narrow(line)
    for j, (own, core, chip, out) in enumerate(
        ((own_ref, core_ref, chip_ref, now_ref), (prev_own_ref, prev_core_ref, prev_chip_ref, prev_ref))
    ):
        both = jnp.concatenate([core[...], chip[...]], axis=0)
        moved = jnp.dot(hit, both, preferred_element_type=F32)
        block = (own[...].astype(F32) + moved).astype(BF16)
        out[...] = block
        for ref, half in ((up_ref, block[:line]), (down_ref, block[line:])):
            sent = jnp.dot(take, half, preferred_element_type=F32).astype(BF16)
            ref[j * sent.shape[0] : (j + 1) * sent.shape[0]] = sent


def fetch_kernel(
    unit,
    parts_ref,
    gain_ref,
    bias_ref,
    b_ref,
    w_ref,
    coef_ref,
    w_out_ref,
    gain_buf,
    bias_buf,
    b_buf,
    small,
    sems,
):
    pairs = ((gain_ref, gain_buf), (bias_ref, bias_buf), (b_ref, b_buf))
    few = [pltpu.make_async_copy(ref, buf, small.at[k]) for k, (ref, buf) in enumerate(pairs)]
    weights = [pltpu.make_async_copy(w_ref.at[a], w_out_ref.at[a], sems.at[a]) for a in range(3)]
    for copy in few + weights:
        copy.start()
    for copy in few:
        copy.wait()
    now, before = affine(parts_ref[...], unit, gain_buf[...], bias_buf[...], lax.axis_index("tm"))
    for k, row in enumerate(now + before):
        coef_ref[k : k + 1] = row
    coef_ref[4:5, : b_buf.shape[1]] = b_buf[...]
    for copy in weights:
        copy.wait()


def position():
    tm, row, col = (lax.axis_index(a) for a in EVERY)
    return tm, row, col


def up_kernel(
    coef_ref, now_ref, prev_ref, above_ref, below_ref, w_ref, w_res_ref, hid_ref, sums_ref, w_res_out_ref, x_ref, acc_ref, sem
):
    ahead = pltpu.make_async_copy(w_res_ref.at[0], w_res_out_ref, sem)
    ahead.start()
    tm, row, col = position()
    last_row, last_col = lax.axis_size("row") - 1, lax.axis_size("col") - 1
    scale, offset, scale_prev, offset_prev = (coef_ref[k : k + 1] for k in range(4))
    depth = scale.shape[-1]
    line = prev_ref.shape[0] // 2
    span = line // SLOTS
    sent = above_ref.shape[0] // 2
    slot = lax.broadcasted_iota(jnp.int32, (line, depth), 0) % SLOTS
    inside = (slot >= jnp.where(col > 0, 0, 1)) & (slot <= jnp.where(col < last_col, 11, 10))
    up, down = row > 0, row < last_row

    def active(piece, a, b, valid):
        v = piece[...]
        if v.shape[0] < line:
            v = jnp.dot(widen(v.shape[0]), v, preferred_element_type=F32)
        v = silu(v.astype(F32) * a + b)
        return jnp.where(inside & valid, v, 0.0).astype(BF16)

    take = narrow(ROWS * SLOTS)

    def place_span(block, part, at, a, b, valid):
        rows = [
            active(above_ref.at[part], a, b, valid & up),
            active(block.at[:line], a, b, valid),
            active(block.at[line:], a, b, valid),
            active(below_ref.at[part], a, b, valid & down),
        ]
        for f in range(span):
            frame = jnp.concatenate([r[f * SLOTS : (f + 1) * SLOTS] for r in rows], axis=0)
            x_ref[at + f] = jnp.dot(take, frame, preferred_element_type=F32).astype(BF16)

    place_span(prev_ref, slice(sent, 2 * sent), 0, scale_prev, offset_prev, tm > 0)
    place_span(now_ref, slice(0, sent), span, scale, offset, tm >= 0)
    acc_ref[...] = jnp.zeros_like(acc_ref)

    frames = 2 * span - 2
    size = frames * CELLS
    width = w_ref.shape[-1]
    up_bias = coef_ref[4:5, :width]
    for b in range(3):

        @pl.when(tm >= 0)
        def _():
            x = jnp.concatenate([x_ref[a : a + frames].reshape(size, depth) for a in range(3)], axis=1)
            z = [
                jnp.dot(x, w_ref[:, b, e].reshape(3 * depth, width), preferred_element_type=F32) for e in range(3)
            ]
            even = pltpu.roll(z[0], 1, 0) + (z[1] + z[2])
            odd = (z[0] + z[1]) + pltpu.roll(z[2], size - 1, 0)
            for p in range(2):
                at = SLOTS + ACROSS * ((b == 0 and p == 0) - (b == 2 and p == 1))
                for q, u in ((0, even), (1, odd)):
                    acc_ref[2 * p + q, at : at + size] += u

    total = jnp.zeros((1, width), F32)
    square = jnp.zeros((1, width), F32)
    cell = lax.broadcasted_iota(jnp.int32, (span * CELLS, width), 0) % CELLS
    r, c = cell // ACROSS, cell % ACROSS
    mine = (r >= 1) & (r <= 2) & (c >= 1) & (c <= 10)
    for k in range(4):
        hidden = (acc_ref[k, SLOTS : SLOTS + size] + up_bias).astype(BF16)
        for f in range(frames):
            hid_ref[f, k * CELLS : (k + 1) * CELLS] = hidden[f * CELLS : (f + 1) * CELLS]
        seen = jnp.where(mine, hidden[size - span * CELLS :].astype(F32), 0.0)
        total = total + jnp.sum(seen, axis=0, keepdims=True)
        square = square + jnp.sum(seen * seen, axis=0, keepdims=True)
    sums_ref[...] = jnp.broadcast_to(packed_sums(total, square), sums_ref.shape)
    ahead.wait()


def gather_matrix():
    m = np.zeros((3, 3, 20, 4, 2, 2, ROWS, ACROSS), np.float32)
    for b in range(3):
        for e in range(3):
            for y in range(4):
                for x in range(20):
                    v, u = y + b - 1, x + e - 1
                    m[b, e, x, y, v % 2, u % 2, v // 2 + 1, u // 2 + 1] = 1.0
    return m.reshape(720, 4 * CELLS)


def res_kernel(unit, parts_ref, gain_ref, bias_ref, b_ref, hid_ref, pick_ref, w_first_ref, w_ref, out_ref, g_ref, t_ref, wbuf, sems):
    copies = [pltpu.make_async_copy(w_ref.at[k + 1], wbuf.at[k], sems.at[k]) for k in range(2)]
    for copy in copies:
        copy.start()
    tm, row, col = position()
    last_row, last_col = lax.axis_size("row") - 1, lax.axis_size("col") - 1
    (scale, offset), (scale_prev, offset_prev) = affine(parts_ref[...], unit, gain_ref[...], bias_ref[...], tm)
    width = scale.shape[-1]
    cell = lax.broadcasted_iota(jnp.int32, (4 * CELLS, width), 0)
    parity, r, slot = cell // CELLS, (cell // ACROSS) % ROWS, cell % ACROSS
    y, x = 2 * (r - 1) + parity // 2, 2 * (slot - 1) + parity % 2
    inside = ((y >= 0) | (row > 0)) & ((y < 4) | (row < last_row)) & ((x >= 0) | (col > 0)) & ((x < 20) | (col < last_col))
    n_now = out_ref.shape[0]
    n_prev = hid_ref.shape[0] - n_now
    area = 80
    for f in range(n_prev + n_now):
        a, b = (scale_prev, offset_prev) if f < n_prev else (scale, offset)
        valid = inside & (tm > 0) if f < n_prev else inside
        v = jnp.where(valid, silu(hid_ref[f].astype(F32) * a + b), 0.0)
        picked = jnp.dot(pick_ref[...], v.astype(BF16), preferred_element_type=F32).astype(BF16)
        for k in range(9):
            g_ref[f * area : (f + 1) * area, k * width : (k + 1) * width] = picked[k * area : (k + 1) * area]

    def part(a, w):
        slab = g_ref[a * area : (a + n_now) * area]
        return jnp.dot(slab, w.reshape(9 * width, width), preferred_element_type=F32)

    t_ref[...] = part(0, w_first_ref[...])

    @pl.when(tm >= 0)
    def _():
        for copy in copies:
            copy.wait()
        total = t_ref[...] + (part(1, wbuf[0]) + part(2, wbuf[1]))
        for f in range(n_now):
            hidden = jnp.dot(pick_ref[4 * area : 5 * area], hid_ref[n_prev + f], preferred_element_type=F32)
            decoded = total[f * area : (f + 1) * area] + b_ref[...] + hidden
            out_ref[f] = decoded.reshape(out_ref.shape[1:]).astype(BF16)


def shifted(value, spans, column):
    n_tm, n_col = lax.axis_size("tm"), lax.axis_size("col")
    route = [(t * n_col + c, (t + spans) % n_tm * n_col + column(c)) for t in range(n_tm) for c in range(n_col)]
    return lax.ppermute(value, ("tm", "col"), route)


def params(mib):
    return pltpu.CompilerParams(vmem_limit_bytes=mib * MIB)


def in_hbm(array):
    return pltpu.with_memory_space_constraint(array, pltpu.HBM)


VM = pl.BlockSpec(memory_space=pltpu.VMEM)
HBM = pl.BlockSpec(memory_space=pltpu.HBM)


def local(features, gain_low, bias_low, w_up, b_up, gain_high, bias_high, w_res, b_res):
    n_tm, n_row, n_col = (lax.axis_size(a) for a in EVERY)
    devices = n_tm * n_row * n_col
    frames, height, across, depth = features.shape
    width = w_up.shape[-1]
    low_unit = float(n_row * n_col * frames * height * across * (depth // GROUPS))
    high_unit = float(n_row * n_col * frames * 4 * height * across * (width // GROUPS))

    block = height * frames * SLOTS
    line = frames * SLOTS
    own, to_core, to_chip = pl.pallas_call(
        lay_out_kernel,
        out_shape=(
            jax.ShapeDtypeStruct((block, depth), BF16),
            jax.ShapeDtypeStruct((16, depth), BF16),
            jax.ShapeDtypeStruct((16, depth), BF16),
        ),
        in_specs=[VM],
        out_specs=(VM,) * 3,
        compiler_params=params(16),
        name="lay_out",
    )(features.transpose(0, 2, 1, 3))
    sums = pl.pallas_call(
        low_sums_kernel,
        out_shape=jax.ShapeDtypeStruct((devices, LANES), F32),
        in_specs=[VM],
        out_specs=VM,
        compiler_params=params(16),
        name="low_sums",
    )(own)
    prev_own = shifted(own, 1, lambda c: c)
    prev_chip = shifted(to_chip, 1, lambda c: (c - 1 + 2 * (c % 2)) % n_col)
    chip = shifted(to_chip, 0, lambda c: (c - 1 + 2 * (c % 2)) % n_col)
    prev_core = shifted(to_core, 1, lambda c: c ^ 1)
    core = shifted(to_core, 0, lambda c: c ^ 1)
    first = (core, chip, prev_core, prev_chip, prev_own)
    sums, first = lax.optimization_barrier((sums, first))
    core, chip, prev_core, prev_chip, prev_own = first
    low_parts = lax.all_to_all(sums, EVERY, 0, 0)
    gl, bl, bu = gain_low.reshape(1, -1), bias_low.reshape(1, -1), b_up.reshape(1, -1)
    gh, bh, br = gain_high.reshape(1, -1), bias_high.reshape(1, -1), b_res.reshape(1, -1)
    now, prev, up, down = pl.pallas_call(
        pack_kernel,
        out_shape=(jax.ShapeDtypeStruct((block, depth), BF16),) * 2
        + (jax.ShapeDtypeStruct((block // 16 * 12, depth), BF16),) * 2,
        in_specs=[VM] * 6,
        out_specs=(VM,) * 4,
        compiler_params=params(16),
        name="pack",
    )(own, core, chip, prev_own, prev_core, prev_chip)
    above = lax.ppermute(down, "row", [(i, (i + 1) % n_row) for i in range(n_row)])
    below = lax.ppermute(up, "row", [(i, (i - 1) % n_row) for i in range(n_row)])
    coef, w_near = pl.pallas_call(
        functools.partial(fetch_kernel, low_unit),
        out_shape=(
            jax.ShapeDtypeStruct((8, depth), F32),
            jax.ShapeDtypeStruct((3, 3, 3, depth, width), BF16),
        ),
        in_specs=[VM] + [HBM] * 4,
        out_specs=(VM,) * 2,
        scratch_shapes=[
            pltpu.VMEM((1, depth), F32),
            pltpu.VMEM((1, depth), F32),
            pltpu.VMEM((1, width), F32),
            pltpu.SemaphoreType.DMA((3,)),
            pltpu.SemaphoreType.DMA((3,)),
        ],
        compiler_params=params(16),
        name="fetch",
    )(low_parts, in_hbm(gl), in_hbm(bl), in_hbm(bu), in_hbm(w_up))
    hidden, high_sums, w_res_near = pl.pallas_call(
        up_kernel,
        out_shape=(
            jax.ShapeDtypeStruct((2 + frames, 4 * CELLS, width), BF16),
            jax.ShapeDtypeStruct((devices, LANES), F32),
            jax.ShapeDtypeStruct((3, 3, width, width), BF16),
        ),
        in_specs=[VM] * 6 + [HBM],
        out_specs=(VM,) * 3,
        scratch_shapes=[
            pltpu.VMEM((2 * frames, CELLS, depth), BF16),
            pltpu.VMEM((4, (2 + frames) * CELLS + 2 * SLOTS, width), F32),
            pltpu.SemaphoreType.DMA,
        ],
        compiler_params=params(20),
        name="up",
    )(coef, now, prev, above, below, w_near, in_hbm(w_res))
    high_parts = lax.all_to_all(high_sums, EVERY, 0, 0)

    area = 4 * height * across
    decoded = pl.pallas_call(
        functools.partial(res_kernel, high_unit),
        out_shape=jax.ShapeDtypeStruct((frames, 2 * across, 2 * height, width), BF16),
        in_specs=[VM] * 7 + [HBM],
        out_specs=VM,
        scratch_shapes=[
            pltpu.VMEM(((2 + frames) * area, 9 * width), BF16),
            pltpu.VMEM((frames * area, width), F32),
            pltpu.VMEM((2, 3, 3, width, width), BF16),
            pltpu.SemaphoreType.DMA((2,)),
        ],
        compiler_params=params(24),
        name="res",
    )(high_parts, gh, bh, br, hidden, jnp.asarray(gather_matrix(), BF16), w_res_near, in_hbm(w_res))
    return decoded.transpose(0, 2, 1, 3)


def solution(mesh):
    in_specs = (P("tm", "row", "col", None), P(), P(), P(), P(), P(), P(), P(), P())
    out_specs = P("tm", "row", "col", None)
    return jax.shard_map(local, mesh=mesh, in_specs=in_specs, out_specs=out_specs, check_vma=False)
```

```python
import functools

import jax
import jax.numpy as jnp
import numpy as np
from jax import lax
from jax.experimental import pallas as pl
from jax.experimental.pallas import tpu as pltpu
from jax.sharding import PartitionSpec as P

GROUPS = 32
LANES = 128
EVERY = ("tm", "row", "col")
HIGHEST = lax.Precision.HIGHEST
F32 = jnp.float32
BF16 = jnp.bfloat16
ROWS, ACROSS, SLOTS = 4, 12, 16
CELLS = ROWS * ACROSS
MIB = 1024 * 1024


def group_of(channel, channels):
    return lax.shift_right_logical(channel, int(np.log2(channels // GROUPS)))


def packed_sums(sums, squares):
    channels = sums.shape[-1]
    shape = (channels, LANES)
    member = group_of(lax.broadcasted_iota(jnp.int32, shape, 0), channels) == lax.broadcasted_iota(jnp.int32, shape, 1)
    both = jnp.concatenate([sums, squares, jnp.zeros((6, channels), F32)], axis=0)
    grouped = jnp.dot(both, member.astype(F32), precision=HIGHEST, preferred_element_type=F32)
    return grouped[0:1] + pltpu.roll(grouped, GROUPS, 1)[1:2]


def affine(parts, unit, gain, bias, span):
    channels = gain.shape[-1]
    spans = lax.axis_size("tm")
    each = parts.shape[0] // spans
    now = jnp.zeros((1, LANES), F32)
    before = jnp.zeros((1, LANES), F32)
    for s in range(spans):
        part = jnp.sum(parts[s * each : (s + 1) * each], axis=0, keepdims=True)
        now = now + jnp.where(s <= span, part, 0.0)
        before = before + jnp.where(s < span, part, 0.0)
    stacked = jnp.concatenate([now, before, jnp.zeros((6, LANES), F32)], axis=0)
    stacked = jnp.concatenate([stacked, pltpu.roll(stacked, LANES - GROUPS, 1)], axis=0)
    shape = (LANES, channels)
    member = group_of(lax.broadcasted_iota(jnp.int32, shape, 1), channels) == lax.broadcasted_iota(jnp.int32, shape, 0)
    spread = jnp.dot(stacked, member.astype(F32), precision=HIGHEST, preferred_element_type=F32)
    result = []
    for k in range(2):
        count = jnp.maximum(span + 1 - k, 1).astype(F32) * unit
        mean = spread[k : k + 1] / count
        var = spread[8 + k : 9 + k] / count - mean * mean
        scale = lax.rsqrt(var + 1e-06) * gain
        result.append((scale, bias - mean * scale))
    return result


def silu(x):
    return x / (1.0 + jnp.exp(-x))


def low_sums_kernel(x_ref, w_ref, sums_ref, w_out_ref, rows_ref, sems):
    weights = pltpu.make_async_copy(w_ref.at[:, 0], w_out_ref, sems.at[0])
    weights.start()
    x = x_ref[...].astype(F32)
    row = packed_sums(jnp.sum(x, axis=0, keepdims=True), jnp.sum(x * x, axis=0, keepdims=True))
    rows_ref[...] = jnp.broadcast_to(row, rows_ref.shape)
    out = pltpu.make_async_copy(rows_ref, sums_ref, sems.at[1])
    out.start()

    @pl.when(lax.axis_index("tm") >= 0)
    def _():
        weights.wait()
        out.wait()


def lay_out_kernel(x_ref, own_ref, to_core_ref, to_chip_ref):
    frames, across, height, channels = x_ref.shape
    x = x_ref[...].astype(F32).reshape(frames * across * height, channels)
    block = height * frames * SLOTS
    shape = (block + 32, x.shape[0])
    to = lax.broadcasted_iota(jnp.int32, shape, 0)
    edge = to - block
    odd = lax.axis_index("col") % 2
    last = (edge < 16).astype(jnp.int32) != odd
    k = jnp.where(to < block, to // SLOTS, edge % 16)
    column = jnp.where(to < block, to % SLOTS - 1, jnp.where(last, across - 1, 0))
    source = ((k % frames) * across + column) * height + k // frames
    hit = (lax.broadcasted_iota(jnp.int32, shape, 1) == source) & (column >= 0) & (column < across) & (k < height * frames)
    moved = jnp.dot(hit.astype(BF16), x.astype(BF16), preferred_element_type=F32).astype(BF16)
    own_ref[...] = moved[:block]
    to_core_ref[...] = moved[block : block + 16]
    to_chip_ref[...] = moved[block + 16 :]


def narrow(rows):
    shape = (rows // 16 * 12, rows)
    to, source = (lax.broadcasted_iota(jnp.int32, shape, d) for d in range(2))
    return (source == to // 12 * SLOTS + to % 12).astype(BF16)


def widen(rows):
    shape = (rows // 12 * 16, rows)
    to, source = (lax.broadcasted_iota(jnp.int32, shape, d) for d in range(2))
    return ((to % SLOTS < 12) & (source == to // SLOTS * 12 + to % SLOTS)).astype(BF16)


def pack_kernel(own_ref, core_ref, chip_ref, prev_own_ref, prev_core_ref, prev_chip_ref, now_ref, prev_ref, up_ref, down_ref):
    rows = own_ref.shape[0]
    line = rows // 2
    shape = (rows, 32)
    to = lax.broadcasted_iota(jnp.int32, shape, 0)
    source = lax.broadcasted_iota(jnp.int32, shape, 1)
    core_slot = jnp.where(lax.axis_index("col") % 2 == 0, 11, 0)
    slot, k = to % SLOTS, to // SLOTS
    hit = (((slot == core_slot) & (source == k)) | ((slot == 11 - core_slot) & (source == 16 + k))).astype(BF16)
    take = narrow(line)
    for j, (own, core, chip, out) in enumerate(
        ((own_ref, core_ref, chip_ref, now_ref), (prev_own_ref, prev_core_ref, prev_chip_ref, prev_ref))
    ):
        both = jnp.concatenate([core[...], chip[...]], axis=0)
        moved = jnp.dot(hit, both, preferred_element_type=F32)
        block = (own[...].astype(F32) + moved).astype(BF16)
        out[...] = block
        for ref, half in ((up_ref, block[:line]), (down_ref, block[line:])):
            sent = jnp.dot(take, half, preferred_element_type=F32).astype(BF16)
            ref[j * sent.shape[0] : (j + 1) * sent.shape[0]] = sent


def position():
    tm, row, col = (lax.axis_index(a) for a in EVERY)
    return tm, row, col


def activated(piece, scale, offset, valid):
    col, last_col = lax.axis_index("col"), lax.axis_size("col") - 1
    slot = lax.broadcasted_iota(jnp.int32, piece.shape, 0) % SLOTS
    inside = (slot >= jnp.where(col > 0, 0, 1)) & (slot <= jnp.where(col < last_col, 11, 10))
    return jnp.where(inside & valid, silu(piece.astype(F32) * scale + offset), 0.0).astype(BF16)


def fetch_kernel(
    unit,
    parts_ref,
    now_ref,
    prev_ref,
    gain_ref,
    bias_ref,
    b_ref,
    w_ref,
    coef_ref,
    act_ref,
    act_prev_ref,
    w_out_ref,
    gain_buf,
    bias_buf,
    b_buf,
    small,
    sems,
):
    pairs = ((gain_ref, gain_buf), (bias_ref, bias_buf), (b_ref, b_buf))
    few = [pltpu.make_async_copy(ref, buf, small.at[k]) for k, (ref, buf) in enumerate(pairs)]
    weights = [pltpu.make_async_copy(w_ref.at[:, b + 1], w_out_ref.at[b], sems.at[b]) for b in range(2)]
    for copy in few + weights:
        copy.start()
    for copy in few:
        copy.wait()
    tm = lax.axis_index("tm")
    now, before = affine(parts_ref[...], unit, gain_buf[...], bias_buf[...], tm)
    for k, row in enumerate(now + before):
        coef_ref[k : k + 1] = row
    coef_ref[4:5, : b_buf.shape[1]] = b_buf[...]
    act_ref[...] = activated(now_ref[...], *now, tm >= 0)
    act_prev_ref[...] = activated(prev_ref[...], *before, tm > 0)

    @pl.when(tm >= 0)
    def _():
        for copy in weights:
            copy.wait()


def up_kernel(
    coef_ref,
    act_ref,
    act_prev_ref,
    above_ref,
    below_ref,
    w_first_ref,
    w_rest_ref,
    w_res_ref,
    hid_ref,
    sums_ref,
    w_res_out_ref,
    x_ref,
    acc_ref,
    sem,
):
    ahead = pltpu.make_async_copy(w_res_ref.at[0], w_res_out_ref, sem)
    ahead.start()
    tm, row, col = position()
    last_row = lax.axis_size("row") - 1
    scale, offset, scale_prev, offset_prev = (coef_ref[k : k + 1] for k in range(4))
    depth = scale.shape[-1]
    line = act_ref.shape[0] // 2
    span = line // SLOTS
    sent = above_ref.shape[0] // 2
    up, down = row > 0, row < last_row

    def active(piece, a, b, valid):
        v = piece[...]
        wide = jnp.dot(widen(v.shape[0]), v, preferred_element_type=F32)
        return activated(wide, a, b, valid)

    take = narrow(ROWS * SLOTS)

    def place_span(block, part, at, a, b, valid):
        rows = [
            active(above_ref.at[part], a, b, valid & up),
            block[:line],
            block[line:],
            active(below_ref.at[part], a, b, valid & down),
        ]
        for f in range(span):
            frame = jnp.concatenate([r[f * SLOTS : (f + 1) * SLOTS] for r in rows], axis=0)
            x_ref[at + f] = jnp.dot(take, frame, preferred_element_type=F32).astype(BF16)

    place_span(act_prev_ref, slice(sent, 2 * sent), 0, scale_prev, offset_prev, tm > 0)
    place_span(act_ref, slice(0, sent), span, scale, offset, tm >= 0)
    acc_ref[0:2, SLOTS : SLOTS + ACROSS] = jnp.zeros((2, ACROSS, acc_ref.shape[-1]), F32)

    frames = 2 * span - 2
    size = frames * CELLS
    width = w_first_ref.shape[-1]
    up_bias = coef_ref[4:5, :width]
    for b in range(3):

        @pl.when(tm >= 0)
        def _():
            taps = w_first_ref if b == 0 else w_rest_ref.at[b - 1]
            x = jnp.concatenate([x_ref[a : a + frames].reshape(size, depth) for a in range(3)], axis=1)
            z = [
                jnp.dot(x, taps[:, e].reshape(3 * depth, width), preferred_element_type=F32) for e in range(3)
            ]
            even = pltpu.roll(z[0], 1, 0) + (z[1] + z[2])
            odd = (z[0] + z[1]) + pltpu.roll(z[2], size - 1, 0)
            for p in range(2):
                at = SLOTS + ACROSS * ((b == 0 and p == 0) - (b == 2 and p == 1))
                for q, u in ((0, even), (1, odd)):
                    k, rows = 2 * p + q, slice(at, at + size)
                    acc_ref[k, rows] = u if b == 0 else acc_ref[k, rows] + u

    total = jnp.zeros((1, width), F32)
    square = jnp.zeros((1, width), F32)
    cell = lax.broadcasted_iota(jnp.int32, (span * CELLS, width), 0) % CELLS
    r, c = cell // ACROSS, cell % ACROSS
    mine = (r >= 1) & (r <= 2) & (c >= 1) & (c <= 10)
    for k in range(4):
        hidden = (acc_ref[k, SLOTS : SLOTS + size] + up_bias).astype(BF16)
        for f in range(frames):
            hid_ref[f, k * CELLS : (k + 1) * CELLS] = hidden[f * CELLS : (f + 1) * CELLS]
        seen = jnp.where(mine, hidden[size - span * CELLS :].astype(F32), 0.0)
        total = total + jnp.sum(seen, axis=0, keepdims=True)
        square = square + jnp.sum(seen * seen, axis=0, keepdims=True)
    sums_ref[...] = jnp.broadcast_to(packed_sums(total, square), sums_ref.shape)
    ahead.wait()


def gather_matrix():
    m = np.zeros((3, 3, 20, 4, 2, 2, ROWS, ACROSS), np.float32)
    for b in range(3):
        for e in range(3):
            for y in range(4):
                for x in range(20):
                    v, u = y + b - 1, x + e - 1
                    m[b, e, x, y, v % 2, u % 2, v // 2 + 1, u // 2 + 1] = 1.0
    return m.reshape(720, 4 * CELLS)


def res_kernel(unit, parts_ref, gain_ref, bias_ref, b_ref, hid_ref, pick_ref, w_first_ref, w_ref, out_ref, g_ref, t_ref, wbuf, sems):
    copies = [pltpu.make_async_copy(w_ref.at[k + 1], wbuf.at[k], sems.at[k]) for k in range(2)]
    for copy in copies:
        copy.start()
    tm, row, col = position()
    last_row, last_col = lax.axis_size("row") - 1, lax.axis_size("col") - 1
    (scale, offset), (scale_prev, offset_prev) = affine(parts_ref[...], unit, gain_ref[...], bias_ref[...], tm)
    width = scale.shape[-1]
    cell = lax.broadcasted_iota(jnp.int32, (4 * CELLS, width), 0)
    parity, r, slot = cell // CELLS, (cell // ACROSS) % ROWS, cell % ACROSS
    y, x = 2 * (r - 1) + parity // 2, 2 * (slot - 1) + parity % 2
    inside = ((y >= 0) | (row > 0)) & ((y < 4) | (row < last_row)) & ((x >= 0) | (col > 0)) & ((x < 20) | (col < last_col))
    n_now = out_ref.shape[0]
    n_prev = hid_ref.shape[0] - n_now
    area = 80
    for f in range(n_prev + n_now):
        a, b = (scale_prev, offset_prev) if f < n_prev else (scale, offset)
        valid = inside & (tm > 0) if f < n_prev else inside
        v = jnp.where(valid, silu(hid_ref[f].astype(F32) * a + b), 0.0)
        picked = jnp.dot(pick_ref[...], v.astype(BF16), preferred_element_type=F32).astype(BF16)
        for k in range(9):
            g_ref[f * area : (f + 1) * area, k * width : (k + 1) * width] = picked[k * area : (k + 1) * area]

    def part(a, w):
        slab = g_ref[a * area : (a + n_now) * area]
        return jnp.dot(slab, w.reshape(9 * width, width), preferred_element_type=F32)

    t_ref[...] = part(0, w_first_ref[...])

    @pl.when(tm >= 0)
    def _():
        for copy in copies:
            copy.wait()
        total = t_ref[...] + (part(1, wbuf[0]) + part(2, wbuf[1]))
        for f in range(n_now):
            hidden = jnp.dot(pick_ref[4 * area : 5 * area], hid_ref[n_prev + f], preferred_element_type=F32)
            decoded = total[f * area : (f + 1) * area] + b_ref[...] + hidden
            out_ref[f] = decoded.reshape(out_ref.shape[1:]).astype(BF16)


def shifted(value, spans, column):
    n_tm, n_col = lax.axis_size("tm"), lax.axis_size("col")
    route = [(t * n_col + c, (t + spans) % n_tm * n_col + column(c)) for t in range(n_tm) for c in range(n_col)]
    return lax.ppermute(value, ("tm", "col"), route)


def params(mib):
    return pltpu.CompilerParams(vmem_limit_bytes=mib * MIB)


def in_hbm(array):
    return pltpu.with_memory_space_constraint(array, pltpu.HBM)


VM = pl.BlockSpec(memory_space=pltpu.VMEM)
HBM = pl.BlockSpec(memory_space=pltpu.HBM)


def local(features, gain_low, bias_low, w_up, b_up, gain_high, bias_high, w_res, b_res):
    n_tm, n_row, n_col = (lax.axis_size(a) for a in EVERY)
    devices = n_tm * n_row * n_col
    frames, height, across, depth = features.shape
    width = w_up.shape[-1]
    low_unit = float(n_row * n_col * frames * height * across * (depth // GROUPS))
    high_unit = float(n_row * n_col * frames * 4 * height * across * (width // GROUPS))

    block = height * frames * SLOTS
    line = frames * SLOTS
    own, to_core, to_chip = pl.pallas_call(
        lay_out_kernel,
        out_shape=(
            jax.ShapeDtypeStruct((block, depth), BF16),
            jax.ShapeDtypeStruct((16, depth), BF16),
            jax.ShapeDtypeStruct((16, depth), BF16),
        ),
        in_specs=[VM],
        out_specs=(VM,) * 3,
        compiler_params=params(16),
        name="lay_out",
    )(features.transpose(0, 2, 1, 3))
    sums, w_first = pl.pallas_call(
        low_sums_kernel,
        out_shape=(jax.ShapeDtypeStruct((devices, LANES), F32), jax.ShapeDtypeStruct((3, 3, depth, width), BF16)),
        in_specs=[VM, HBM],
        out_specs=(HBM, VM),
        scratch_shapes=[pltpu.VMEM((devices, LANES), F32), pltpu.SemaphoreType.DMA((2,))],
        compiler_params=params(16),
        name="low_sums",
    )(own, in_hbm(w_up))
    prev_own = shifted(own, 1, lambda c: c)
    prev_chip = shifted(to_chip, 1, lambda c: (c - 1 + 2 * (c % 2)) % n_col)
    chip = shifted(to_chip, 0, lambda c: (c - 1 + 2 * (c % 2)) % n_col)
    prev_core = shifted(to_core, 1, lambda c: c ^ 1)
    core = shifted(to_core, 0, lambda c: c ^ 1)
    first = (core, chip, prev_core, prev_chip, prev_own)
    sums, first = lax.optimization_barrier((sums, first))
    core, chip, prev_core, prev_chip, prev_own = first
    low_parts = lax.all_to_all(sums, EVERY, 0, 0)
    gl, bl, bu = gain_low.reshape(1, -1), bias_low.reshape(1, -1), b_up.reshape(1, -1)
    gh, bh, br = gain_high.reshape(1, -1), bias_high.reshape(1, -1), b_res.reshape(1, -1)
    now, prev, up, down = pl.pallas_call(
        pack_kernel,
        out_shape=(jax.ShapeDtypeStruct((block, depth), BF16),) * 2
        + (jax.ShapeDtypeStruct((block // 16 * 12, depth), BF16),) * 2,
        in_specs=[VM] * 6,
        out_specs=(VM,) * 4,
        compiler_params=params(16),
        name="pack",
    )(own, core, chip, prev_own, prev_core, prev_chip)
    above = lax.ppermute(down, "row", [(i, (i + 1) % n_row) for i in range(n_row)])
    below = lax.ppermute(up, "row", [(i, (i - 1) % n_row) for i in range(n_row)])
    coef, act, act_prev, w_rest = pl.pallas_call(
        functools.partial(fetch_kernel, low_unit),
        out_shape=(
            jax.ShapeDtypeStruct((8, depth), F32),
            jax.ShapeDtypeStruct((block, depth), BF16),
            jax.ShapeDtypeStruct((block, depth), BF16),
            jax.ShapeDtypeStruct((2, 3, 3, depth, width), BF16),
        ),
        in_specs=[VM] * 3 + [HBM] * 4,
        out_specs=(VM,) * 4,
        scratch_shapes=[
            pltpu.VMEM((1, depth), F32),
            pltpu.VMEM((1, depth), F32),
            pltpu.VMEM((1, width), F32),
            pltpu.SemaphoreType.DMA((3,)),
            pltpu.SemaphoreType.DMA((2,)),
        ],
        compiler_params=params(16),
        name="fetch",
    )(low_parts, now, prev, in_hbm(gl), in_hbm(bl), in_hbm(bu), in_hbm(w_up))
    hidden, high_sums, w_res_near = pl.pallas_call(
        up_kernel,
        out_shape=(
            jax.ShapeDtypeStruct((2 + frames, 4 * CELLS, width), BF16),
            jax.ShapeDtypeStruct((devices, LANES), F32),
            jax.ShapeDtypeStruct((3, 3, width, width), BF16),
        ),
        in_specs=[VM] * 7 + [HBM],
        out_specs=(VM,) * 3,
        scratch_shapes=[
            pltpu.VMEM((2 * frames, CELLS, depth), BF16),
            pltpu.VMEM((4, (2 + frames) * CELLS + 2 * SLOTS, width), F32),
            pltpu.SemaphoreType.DMA,
        ],
        compiler_params=params(20),
        name="up",
    )(coef, act, act_prev, above, below, w_first, w_rest, in_hbm(w_res))
    high_parts = lax.all_to_all(high_sums, EVERY, 0, 0)

    area = 4 * height * across
    decoded = pl.pallas_call(
        functools.partial(res_kernel, high_unit),
        out_shape=jax.ShapeDtypeStruct((frames, 2 * across, 2 * height, width), BF16),
        in_specs=[VM] * 7 + [HBM],
        out_specs=VM,
        scratch_shapes=[
            pltpu.VMEM(((2 + frames) * area, 9 * width), BF16),
            pltpu.VMEM((frames * area, width), F32),
            pltpu.VMEM((2, 3, 3, width, width), BF16),
            pltpu.SemaphoreType.DMA((2,)),
        ],
        compiler_params=params(24),
        name="res",
    )(high_parts, gh, bh, br, hidden, jnp.asarray(gather_matrix(), BF16), w_res_near, in_hbm(w_res))
    return decoded.transpose(0, 2, 1, 3)


def solution(mesh):
    in_specs = (P("tm", "row", "col", None), P(), P(), P(), P(), P(), P(), P(), P())
    out_specs = P("tm", "row", "col", None)
    return jax.shard_map(local, mesh=mesh, in_specs=in_specs, out_specs=out_specs, check_vma=False)
```

```python
import functools

import jax
import jax.numpy as jnp
import numpy as np
from jax import lax
from jax.experimental import pallas as pl
from jax.experimental.pallas import tpu as pltpu
from jax.sharding import PartitionSpec as P

GROUPS = 32
LANES = 128
EVERY = ("tm", "row", "col")
HIGHEST = lax.Precision.HIGHEST
F32 = jnp.float32
BF16 = jnp.bfloat16
ROWS, ACROSS, SLOTS = 4, 12, 16
CELLS = ROWS * ACROSS
MIB = 1024 * 1024


def group_of(channel, channels):
    return lax.shift_right_logical(channel, int(np.log2(channels // GROUPS)))


def packed_sums(sums, squares):
    channels = sums.shape[-1]
    shape = (channels, LANES)
    member = group_of(lax.broadcasted_iota(jnp.int32, shape, 0), channels) == lax.broadcasted_iota(jnp.int32, shape, 1)
    both = jnp.concatenate([sums, squares, jnp.zeros((6, channels), F32)], axis=0)
    grouped = jnp.dot(both, member.astype(F32), precision=HIGHEST, preferred_element_type=F32)
    return grouped[0:1] + pltpu.roll(grouped, GROUPS, 1)[1:2]


def affine(parts, unit, gain, bias, span):
    channels = gain.shape[-1]
    spans = lax.axis_size("tm")
    each = parts.shape[0] // spans
    now = jnp.zeros((1, LANES), F32)
    before = jnp.zeros((1, LANES), F32)
    for s in range(spans):
        part = jnp.sum(parts[s * each : (s + 1) * each], axis=0, keepdims=True)
        now = now + jnp.where(s <= span, part, 0.0)
        before = before + jnp.where(s < span, part, 0.0)
    stacked = jnp.concatenate([now, before, jnp.zeros((6, LANES), F32)], axis=0)
    stacked = jnp.concatenate([stacked, pltpu.roll(stacked, LANES - GROUPS, 1)], axis=0)
    shape = (LANES, channels)
    member = group_of(lax.broadcasted_iota(jnp.int32, shape, 1), channels) == lax.broadcasted_iota(jnp.int32, shape, 0)
    spread = jnp.dot(stacked, member.astype(F32), precision=HIGHEST, preferred_element_type=F32)
    result = []
    for k in range(2):
        count = jnp.maximum(span + 1 - k, 1).astype(F32) * unit
        mean = spread[k : k + 1] / count
        var = spread[8 + k : 9 + k] / count - mean * mean
        scale = lax.rsqrt(var + 1e-06) * gain
        result.append((scale, bias - mean * scale))
    return result


def silu(x):
    half = 0.5 * x
    return half + half * jnp.tanh(half)


def by_twelve(n):
    quotient = lax.shift_right_logical(n * 171, 11)
    return quotient, n - 12 * quotient


def low_sums_kernel(x_ref, w_ref, sums_ref, w_out_ref, rows_ref, sems):
    weights = pltpu.make_async_copy(w_ref.at[:, 0], w_out_ref, sems.at[0])
    weights.start()
    x = x_ref[...].astype(F32)
    row = packed_sums(jnp.sum(x, axis=0, keepdims=True), jnp.sum(x * x, axis=0, keepdims=True))
    rows_ref[...] = jnp.broadcast_to(row, rows_ref.shape)
    out = pltpu.make_async_copy(rows_ref, sums_ref, sems.at[1])
    out.start()

    @pl.when(lax.axis_index("tm") >= 0)
    def _():
        weights.wait()
        out.wait()


def lay_out_kernel(x_ref, own_ref, to_core_ref, to_chip_ref):
    frames, across, height, channels = x_ref.shape
    x = x_ref[...].astype(F32).reshape(frames * across * height, channels)
    block = height * frames * SLOTS
    shape = (block + 32, x.shape[0])
    to = lax.broadcasted_iota(jnp.int32, shape, 0)
    edge = to - block
    odd = lax.axis_index("col") % 2
    last = (edge < 16).astype(jnp.int32) != odd
    k = jnp.where(to < block, to // SLOTS, edge % 16)
    column = jnp.where(to < block, to % SLOTS - 1, jnp.where(last, across - 1, 0))
    source = ((k % frames) * across + column) * height + k // frames
    hit = (lax.broadcasted_iota(jnp.int32, shape, 1) == source) & (column >= 0) & (column < across) & (k < height * frames)
    moved = jnp.dot(hit.astype(BF16), x.astype(BF16), preferred_element_type=F32).astype(BF16)
    own_ref[...] = moved[:block]
    to_core_ref[...] = moved[block : block + 16]
    to_chip_ref[...] = moved[block + 16 :]


def narrow(rows):
    shape = (rows // 16 * 12, rows)
    to, source = (lax.broadcasted_iota(jnp.int32, shape, d) for d in range(2))
    quotient, rest = by_twelve(to)
    return (source == quotient * SLOTS + rest).astype(BF16)


def widen(rows):
    shape = (rows // 12 * 16, rows)
    to, source = (lax.broadcasted_iota(jnp.int32, shape, d) for d in range(2))
    slot = to & (SLOTS - 1)
    return ((slot < 12) & (source == lax.shift_right_logical(to, 4) * 12 + slot)).astype(BF16)


def pack_kernel(own_ref, core_ref, chip_ref, prev_own_ref, prev_core_ref, prev_chip_ref, now_ref, prev_ref, up_ref, down_ref):
    rows = own_ref.shape[0]
    line = rows // 2
    shape = (rows, 32)
    to = lax.broadcasted_iota(jnp.int32, shape, 0)
    source = lax.broadcasted_iota(jnp.int32, shape, 1)
    core_slot = jnp.where(lax.axis_index("col") % 2 == 0, 11, 0)
    slot, k = to & (SLOTS - 1), lax.shift_right_logical(to, 4)
    hit = (((slot == core_slot) & (source == k)) | ((slot == 11 - core_slot) & (source == 16 + k))).astype(BF16)
    take = narrow(line)
    for j, (own, core, chip, out) in enumerate(
        ((own_ref, core_ref, chip_ref, now_ref), (prev_own_ref, prev_core_ref, prev_chip_ref, prev_ref))
    ):
        both = jnp.concatenate([core[...], chip[...]], axis=0)
        moved = jnp.dot(hit, both, preferred_element_type=F32)
        block = (own[...].astype(F32) + moved).astype(BF16)
        out[...] = block
        for ref, half in ((up_ref, block[:line]), (down_ref, block[line:])):
            sent = jnp.dot(take, half, preferred_element_type=F32).astype(BF16)
            ref[j * sent.shape[0] : (j + 1) * sent.shape[0]] = sent


def position():
    tm, row, col = (lax.axis_index(a) for a in EVERY)
    return tm, row, col


def activated(piece, scale, offset, valid):
    col, last_col = lax.axis_index("col"), lax.axis_size("col") - 1
    slot = lax.broadcasted_iota(jnp.int32, piece.shape, 0) & (SLOTS - 1)
    inside = (slot >= jnp.where(col > 0, 0, 1)) & (slot <= jnp.where(col < last_col, 11, 10))
    return jnp.where(inside & valid, silu(piece.astype(F32) * scale + offset), 0.0).astype(BF16)


def fetch_kernel(
    unit,
    parts_ref,
    now_ref,
    prev_ref,
    gain_ref,
    bias_ref,
    b_ref,
    w_ref,
    coef_ref,
    act_ref,
    act_prev_ref,
    w_out_ref,
    gain_buf,
    bias_buf,
    b_buf,
    small,
    sems,
):
    pairs = ((gain_ref, gain_buf), (bias_ref, bias_buf), (b_ref, b_buf))
    few = [pltpu.make_async_copy(ref, buf, small.at[k]) for k, (ref, buf) in enumerate(pairs)]
    weights = [pltpu.make_async_copy(w_ref.at[:, b + 1], w_out_ref.at[b], sems.at[b]) for b in range(2)]
    for copy in few + weights:
        copy.start()
    for copy in few:
        copy.wait()
    tm = lax.axis_index("tm")
    now, before = affine(parts_ref[...], unit, gain_buf[...], bias_buf[...], tm)
    for k, row in enumerate(now + before):
        coef_ref[k : k + 1] = row
    coef_ref[4:5, : b_buf.shape[1]] = b_buf[...]
    act_ref[...] = activated(now_ref[...], *now, tm >= 0)
    act_prev_ref[...] = activated(prev_ref[...], *before, tm > 0)

    @pl.when(tm >= 0)
    def _():
        for copy in weights:
            copy.wait()


def up_kernel(
    coef_ref,
    act_ref,
    act_prev_ref,
    above_ref,
    below_ref,
    w_first_ref,
    w_rest_ref,
    w_res_ref,
    hid_ref,
    sums_ref,
    w_res_out_ref,
    x_ref,
    acc_ref,
    sem,
):
    ahead = pltpu.make_async_copy(w_res_ref.at[0], w_res_out_ref, sem)
    ahead.start()
    tm, row, col = position()
    last_row = lax.axis_size("row") - 1
    scale, offset, scale_prev, offset_prev = (coef_ref[k : k + 1] for k in range(4))
    depth = scale.shape[-1]
    line = act_ref.shape[0] // 2
    span = line // SLOTS
    sent = above_ref.shape[0] // 2
    up, down = row > 0, row < last_row

    def active(piece, a, b, valid):
        v = piece[...]
        wide = jnp.dot(widen(v.shape[0]), v, preferred_element_type=F32)
        return activated(wide, a, b, valid)

    take = narrow(ROWS * SLOTS)

    def place_span(block, part, at, a, b, valid):
        rows = [
            active(above_ref.at[part], a, b, valid & up),
            block[:line],
            block[line:],
            active(below_ref.at[part], a, b, valid & down),
        ]
        for f in range(span):
            frame = jnp.concatenate([r[f * SLOTS : (f + 1) * SLOTS] for r in rows], axis=0)
            x_ref[at + f] = jnp.dot(take, frame, preferred_element_type=F32).astype(BF16)

    place_span(act_prev_ref, slice(sent, 2 * sent), 0, scale_prev, offset_prev, tm > 0)
    place_span(act_ref, slice(0, sent), span, scale, offset, tm >= 0)
    acc_ref[0:2, SLOTS : SLOTS + ACROSS] = jnp.zeros((2, ACROSS, acc_ref.shape[-1]), F32)

    frames = 2 * span - 2
    size = frames * CELLS
    width = w_first_ref.shape[-1]
    up_bias = coef_ref[4:5, :width]
    for b in range(3):

        @pl.when(tm >= 0)
        def _():
            taps = w_first_ref if b == 0 else w_rest_ref.at[b - 1]
            x = jnp.concatenate([x_ref[a : a + frames].reshape(size, depth) for a in range(3)], axis=1)
            z = [
                jnp.dot(x, taps[:, e].reshape(3 * depth, width), preferred_element_type=F32) for e in range(3)
            ]
            even = pltpu.roll(z[0], 1, 0) + (z[1] + z[2])
            odd = (z[0] + z[1]) + pltpu.roll(z[2], size - 1, 0)
            for p in range(2):
                at = SLOTS + ACROSS * ((b == 0 and p == 0) - (b == 2 and p == 1))
                for q, u in ((0, even), (1, odd)):
                    k, rows = 2 * p + q, slice(at, at + size)
                    acc_ref[k, rows] = u if b == 0 else acc_ref[k, rows] + u

    total = jnp.zeros((1, width), F32)
    square = jnp.zeros((1, width), F32)
    line_of, c = by_twelve(lax.broadcasted_iota(jnp.int32, (span * CELLS, width), 0))
    r = line_of & (ROWS - 1)
    mine = (r >= 1) & (r <= 2) & (c >= 1) & (c <= 10)
    for k in range(4):
        hidden = (acc_ref[k, SLOTS : SLOTS + size] + up_bias).astype(BF16)
        for f in range(frames):
            hid_ref[f, k * CELLS : (k + 1) * CELLS] = hidden[f * CELLS : (f + 1) * CELLS]
        seen = jnp.where(mine, hidden[size - span * CELLS :].astype(F32), 0.0)
        total = total + jnp.sum(seen, axis=0, keepdims=True)
        square = square + jnp.sum(seen * seen, axis=0, keepdims=True)
    sums_ref[...] = jnp.broadcast_to(packed_sums(total, square), sums_ref.shape)
    ahead.wait()


def gather_matrix():
    m = np.zeros((3, 3, 20, 4, 2, 2, ROWS, ACROSS), np.float32)
    for b in range(3):
        for e in range(3):
            for y in range(4):
                for x in range(20):
                    v, u = y + b - 1, x + e - 1
                    m[b, e, x, y, v % 2, u % 2, v // 2 + 1, u // 2 + 1] = 1.0
    return m.reshape(720, 4 * CELLS)


def res_kernel(unit, parts_ref, gain_ref, bias_ref, b_ref, hid_ref, pick_ref, w_first_ref, w_ref, out_ref, g_ref, t_ref, wbuf, sems):
    copies = [pltpu.make_async_copy(w_ref.at[k + 1], wbuf.at[k], sems.at[k]) for k in range(2)]
    for copy in copies:
        copy.start()
    tm, row, col = position()
    last_row, last_col = lax.axis_size("row") - 1, lax.axis_size("col") - 1
    (scale, offset), (scale_prev, offset_prev) = affine(parts_ref[...], unit, gain_ref[...], bias_ref[...], tm)
    width = scale.shape[-1]
    line_of, slot = by_twelve(lax.broadcasted_iota(jnp.int32, (4 * CELLS, width), 0))
    parity, r = lax.shift_right_logical(line_of, 2), line_of & (ROWS - 1)
    y, x = 2 * (r - 1) + lax.shift_right_logical(parity, 1), 2 * (slot - 1) + (parity & 1)
    inside = ((y >= 0) | (row > 0)) & ((y < 4) | (row < last_row)) & ((x >= 0) | (col > 0)) & ((x < 20) | (col < last_col))
    n_now = out_ref.shape[0]
    n_prev = hid_ref.shape[0] - n_now
    area = 80
    for f in range(n_prev + n_now):
        a, b = (scale_prev, offset_prev) if f < n_prev else (scale, offset)
        valid = inside & (tm > 0) if f < n_prev else inside
        v = jnp.where(valid, silu(hid_ref[f].astype(F32) * a + b), 0.0)
        picked = jnp.dot(pick_ref[...], v.astype(BF16), preferred_element_type=F32).astype(BF16)
        for k in range(9):
            g_ref[f * area : (f + 1) * area, k * width : (k + 1) * width] = picked[k * area : (k + 1) * area]

    def part(a, w):
        slab = g_ref[a * area : (a + n_now) * area]
        return jnp.dot(slab, w.reshape(9 * width, width), preferred_element_type=F32)

    t_ref[...] = part(0, w_first_ref[...])

    @pl.when(tm >= 0)
    def _():
        for copy in copies:
            copy.wait()
        total = t_ref[...] + (part(1, wbuf[0]) + part(2, wbuf[1]))
        for f in range(n_now):
            hidden = jnp.dot(pick_ref[4 * area : 5 * area], hid_ref[n_prev + f], preferred_element_type=F32)
            decoded = total[f * area : (f + 1) * area] + b_ref[...] + hidden
            out_ref[f] = decoded.reshape(out_ref.shape[1:]).astype(BF16)


def shifted(value, spans, column):
    n_tm, n_col = lax.axis_size("tm"), lax.axis_size("col")
    route = [(t * n_col + c, (t + spans) % n_tm * n_col + column(c)) for t in range(n_tm) for c in range(n_col)]
    return lax.ppermute(value, ("tm", "col"), route)


def params(mib):
    return pltpu.CompilerParams(vmem_limit_bytes=mib * MIB)


def in_hbm(array):
    return pltpu.with_memory_space_constraint(array, pltpu.HBM)


VM = pl.BlockSpec(memory_space=pltpu.VMEM)
HBM = pl.BlockSpec(memory_space=pltpu.HBM)


def local(features, gain_low, bias_low, w_up, b_up, gain_high, bias_high, w_res, b_res):
    n_tm, n_row, n_col = (lax.axis_size(a) for a in EVERY)
    devices = n_tm * n_row * n_col
    frames, height, across, depth = features.shape
    width = w_up.shape[-1]
    low_unit = float(n_row * n_col * frames * height * across * (depth // GROUPS))
    high_unit = float(n_row * n_col * frames * 4 * height * across * (width // GROUPS))

    block = height * frames * SLOTS
    line = frames * SLOTS
    own, to_core, to_chip = pl.pallas_call(
        lay_out_kernel,
        out_shape=(
            jax.ShapeDtypeStruct((block, depth), BF16),
            jax.ShapeDtypeStruct((16, depth), BF16),
            jax.ShapeDtypeStruct((16, depth), BF16),
        ),
        in_specs=[VM],
        out_specs=(VM,) * 3,
        compiler_params=params(16),
        name="lay_out",
    )(features.transpose(0, 2, 1, 3))
    sums, w_first = pl.pallas_call(
        low_sums_kernel,
        out_shape=(jax.ShapeDtypeStruct((devices, LANES), F32), jax.ShapeDtypeStruct((3, 3, depth, width), BF16)),
        in_specs=[VM, HBM],
        out_specs=(HBM, VM),
        scratch_shapes=[pltpu.VMEM((devices, LANES), F32), pltpu.SemaphoreType.DMA((2,))],
        compiler_params=params(16),
        name="low_sums",
    )(own, in_hbm(w_up))
    prev_own = shifted(own, 1, lambda c: c)
    prev_core = shifted(to_core, 1, lambda c: c ^ 1)
    core = shifted(to_core, 0, lambda c: c ^ 1)
    prev_chip = shifted(to_chip, 1, lambda c: (c - 1 + 2 * (c % 2)) % n_col)
    chip = shifted(to_chip, 0, lambda c: (c - 1 + 2 * (c % 2)) % n_col)
    first = (chip, core, prev_chip, prev_core, prev_own)
    sums, first = lax.optimization_barrier((sums, first))
    chip, core, prev_chip, prev_core, prev_own = first
    low_parts = lax.all_to_all(sums, EVERY, 0, 0)
    gl, bl, bu = gain_low.reshape(1, -1), bias_low.reshape(1, -1), b_up.reshape(1, -1)
    gh, bh, br = gain_high.reshape(1, -1), bias_high.reshape(1, -1), b_res.reshape(1, -1)
    now, prev, up, down = pl.pallas_call(
        pack_kernel,
        out_shape=(jax.ShapeDtypeStruct((block, depth), BF16),) * 2
        + (jax.ShapeDtypeStruct((block // 16 * 12, depth), BF16),) * 2,
        in_specs=[VM] * 6,
        out_specs=(VM,) * 4,
        compiler_params=params(16),
        name="pack",
    )(own, core, chip, prev_own, prev_core, prev_chip)
    above = lax.ppermute(down, "row", [(i, (i + 1) % n_row) for i in range(n_row)])
    below = lax.ppermute(up, "row", [(i, (i - 1) % n_row) for i in range(n_row)])
    coef, act, act_prev, w_rest = pl.pallas_call(
        functools.partial(fetch_kernel, low_unit),
        out_shape=(
            jax.ShapeDtypeStruct((8, depth), F32),
            jax.ShapeDtypeStruct((block, depth), BF16),
            jax.ShapeDtypeStruct((block, depth), BF16),
            jax.ShapeDtypeStruct((2, 3, 3, depth, width), BF16),
        ),
        in_specs=[VM] * 3 + [HBM] * 4,
        out_specs=(VM,) * 4,
        scratch_shapes=[
            pltpu.VMEM((1, depth), F32),
            pltpu.VMEM((1, depth), F32),
            pltpu.VMEM((1, width), F32),
            pltpu.SemaphoreType.DMA((3,)),
            pltpu.SemaphoreType.DMA((2,)),
        ],
        compiler_params=params(16),
        name="fetch",
    )(low_parts, now, prev, in_hbm(gl), in_hbm(bl), in_hbm(bu), in_hbm(w_up))
    hidden, high_sums, w_res_near = pl.pallas_call(
        up_kernel,
        out_shape=(
            jax.ShapeDtypeStruct((2 + frames, 4 * CELLS, width), BF16),
            jax.ShapeDtypeStruct((devices, LANES), F32),
            jax.ShapeDtypeStruct((3, 3, width, width), BF16),
        ),
        in_specs=[VM] * 7 + [HBM],
        out_specs=(VM,) * 3,
        scratch_shapes=[
            pltpu.VMEM((2 * frames, CELLS, depth), BF16),
            pltpu.VMEM((4, (2 + frames) * CELLS + 2 * SLOTS, width), F32),
            pltpu.SemaphoreType.DMA,
        ],
        compiler_params=params(20),
        name="up",
    )(coef, act, act_prev, above, below, w_first, w_rest, in_hbm(w_res))
    high_parts = lax.all_to_all(high_sums, EVERY, 0, 0)

    area = 4 * height * across
    decoded = pl.pallas_call(
        functools.partial(res_kernel, high_unit),
        out_shape=jax.ShapeDtypeStruct((frames, 2 * across, 2 * height, width), BF16),
        in_specs=[VM] * 7 + [HBM],
        out_specs=VM,
        scratch_shapes=[
            pltpu.VMEM(((2 + frames) * area, 9 * width), BF16),
            pltpu.VMEM((frames * area, width), F32),
            pltpu.VMEM((2, 3, 3, width, width), BF16),
            pltpu.SemaphoreType.DMA((2,)),
        ],
        compiler_params=params(24),
        name="res",
    )(high_parts, gh, bh, br, hidden, jnp.asarray(gather_matrix(), BF16), w_res_near, in_hbm(w_res))
    return decoded.transpose(0, 2, 1, 3)


def solution(mesh):
    in_specs = (P("tm", "row", "col", None), P(), P(), P(), P(), P(), P(), P(), P())
    out_specs = P("tm", "row", "col", None)
    return jax.shard_map(local, mesh=mesh, in_specs=in_specs, out_specs=out_specs, check_vma=False)
```

```python
import functools

import jax
import jax.numpy as jnp
import numpy as np
from jax import lax
from jax.experimental import pallas as pl
from jax.experimental.pallas import tpu as pltpu
from jax.sharding import PartitionSpec as P

GROUPS = 32
LANES = 128
EVERY = ("tm", "row", "col")
HIGHEST = lax.Precision.HIGHEST
F32 = jnp.float32
BF16 = jnp.bfloat16
ROWS, ACROSS, SLOTS = 4, 12, 16
CELLS = ROWS * ACROSS
MIB = 1024 * 1024


def group_of(channel, channels):
    return lax.shift_right_logical(channel, int(np.log2(channels // GROUPS)))


def packed_sums(sums, squares):
    channels = sums.shape[-1]
    shape = (channels, LANES)
    member = group_of(lax.broadcasted_iota(jnp.int32, shape, 0), channels) == lax.broadcasted_iota(jnp.int32, shape, 1)
    both = jnp.concatenate([sums, squares, jnp.zeros((6, channels), F32)], axis=0)
    grouped = jnp.dot(both, member.astype(F32), precision=HIGHEST, preferred_element_type=F32)
    return grouped[0:1] + pltpu.roll(grouped, GROUPS, 1)[1:2]


def affine(parts, unit, gain, bias, span):
    channels = gain.shape[-1]
    spans = lax.axis_size("tm")
    each = parts.shape[0] // spans
    now = jnp.zeros((1, LANES), F32)
    before = jnp.zeros((1, LANES), F32)
    for s in range(spans):
        part = jnp.sum(parts[s * each : (s + 1) * each], axis=0, keepdims=True)
        now = now + jnp.where(s <= span, part, 0.0)
        before = before + jnp.where(s < span, part, 0.0)
    stacked = jnp.concatenate([now, before, jnp.zeros((6, LANES), F32)], axis=0)
    stacked = jnp.concatenate([stacked, pltpu.roll(stacked, LANES - GROUPS, 1)], axis=0)
    shape = (LANES, channels)
    member = group_of(lax.broadcasted_iota(jnp.int32, shape, 1), channels) == lax.broadcasted_iota(jnp.int32, shape, 0)
    spread = jnp.dot(stacked, member.astype(F32), precision=HIGHEST, preferred_element_type=F32)
    result = []
    for k in range(2):
        count = jnp.maximum(span + 1 - k, 1).astype(F32) * unit
        mean = spread[k : k + 1] / count
        var = spread[8 + k : 9 + k] / count - mean * mean
        scale = lax.rsqrt(var + 1e-06) * gain
        result.append((scale, bias - mean * scale))
    return result


def silu(x):
    half = 0.5 * x
    return half + half * jnp.tanh(half)


def by_twelve(n):
    quotient = lax.shift_right_logical(n * 171, 11)
    return quotient, n - 12 * quotient


def low_sums_kernel(x_ref, w_ref, sums_ref, w_out_ref, rows_ref, sems):
    weights = pltpu.make_async_copy(w_ref.at[:, 0], w_out_ref, sems.at[0])
    weights.start()
    x = x_ref[...].astype(F32)
    row = packed_sums(jnp.sum(x, axis=0, keepdims=True), jnp.sum(x * x, axis=0, keepdims=True))
    rows_ref[...] = jnp.broadcast_to(row, rows_ref.shape)
    out = pltpu.make_async_copy(rows_ref, sums_ref, sems.at[1])
    out.start()

    @pl.when(lax.axis_index("tm") >= 0)
    def _():
        weights.wait()
        out.wait()


def lay_out_kernel(x_ref, own_ref, to_core_ref, to_chip_ref):
    frames, across, height, channels = x_ref.shape
    x = x_ref[...].astype(F32).reshape(frames * across * height, channels)
    block = height * frames * SLOTS
    shape = (block + 32, x.shape[0])
    to = lax.broadcasted_iota(jnp.int32, shape, 0)
    edge = to - block
    odd = lax.axis_index("col") % 2
    last = (edge < 16).astype(jnp.int32) != odd
    k = jnp.where(to < block, to // SLOTS, edge % 16)
    column = jnp.where(to < block, to % SLOTS - 1, jnp.where(last, across - 1, 0))
    source = ((k % frames) * across + column) * height + k // frames
    hit = (lax.broadcasted_iota(jnp.int32, shape, 1) == source) & (column >= 0) & (column < across) & (k < height * frames)
    moved = jnp.dot(hit.astype(BF16), x.astype(BF16), preferred_element_type=F32).astype(BF16)
    own_ref[...] = moved[:block]
    to_core_ref[...] = moved[block : block + 16]
    to_chip_ref[...] = moved[block + 16 :]


def narrow(rows):
    shape = (rows // 16 * 12, rows)
    to, source = (lax.broadcasted_iota(jnp.int32, shape, d) for d in range(2))
    quotient, rest = by_twelve(to)
    return (source == quotient * SLOTS + rest).astype(BF16)


def pack_kernel(own_ref, core_ref, chip_ref, prev_own_ref, prev_core_ref, prev_chip_ref, now_ref, prev_ref, up_ref, down_ref):
    rows = own_ref.shape[0]
    line = rows // 2
    shape = (rows, 32)
    to = lax.broadcasted_iota(jnp.int32, shape, 0)
    source = lax.broadcasted_iota(jnp.int32, shape, 1)
    core_slot = jnp.where(lax.axis_index("col") % 2 == 0, 11, 0)
    slot, k = to & (SLOTS - 1), lax.shift_right_logical(to, 4)
    hit = (((slot == core_slot) & (source == k)) | ((slot == 11 - core_slot) & (source == 16 + k))).astype(BF16)
    for j, (own, core, chip, out) in enumerate(
        ((own_ref, core_ref, chip_ref, now_ref), (prev_own_ref, prev_core_ref, prev_chip_ref, prev_ref))
    ):
        both = jnp.concatenate([core[...], chip[...]], axis=0)
        moved = jnp.dot(hit, both, preferred_element_type=F32)
        block = (own[...].astype(F32) + moved).astype(BF16)
        out[...] = block
        for ref, half in ((up_ref, block[:line]), (down_ref, block[line:])):
            ref[j * line : (j + 1) * line] = half


def position():
    tm, row, col = (lax.axis_index(a) for a in EVERY)
    return tm, row, col


def activated(piece, scale, offset, valid):
    col, last_col = lax.axis_index("col"), lax.axis_size("col") - 1
    slot = lax.broadcasted_iota(jnp.int32, piece.shape, 0) & (SLOTS - 1)
    inside = (slot >= jnp.where(col > 0, 0, 1)) & (slot <= jnp.where(col < last_col, 11, 10))
    return jnp.where(inside & valid, silu(piece.astype(F32) * scale + offset), 0.0).astype(BF16)


def fetch_kernel(
    unit,
    parts_ref,
    now_ref,
    prev_ref,
    gain_ref,
    bias_ref,
    b_ref,
    w_ref,
    coef_ref,
    act_ref,
    act_prev_ref,
    w_out_ref,
    gain_buf,
    bias_buf,
    b_buf,
    small,
    sems,
):
    pairs = ((gain_ref, gain_buf), (bias_ref, bias_buf), (b_ref, b_buf))
    few = [pltpu.make_async_copy(ref, buf, small.at[k]) for k, (ref, buf) in enumerate(pairs)]
    weights = [pltpu.make_async_copy(w_ref.at[:, b + 1], w_out_ref.at[b], sems.at[b]) for b in range(2)]
    for copy in few + weights:
        copy.start()
    for copy in few:
        copy.wait()
    tm = lax.axis_index("tm")
    now, before = affine(parts_ref[...], unit, gain_buf[...], bias_buf[...], tm)
    for k, row in enumerate(now + before):
        coef_ref[k : k + 1] = row
    coef_ref[4:5, : b_buf.shape[1]] = b_buf[...]
    act_ref[...] = activated(now_ref[...], *now, tm >= 0)
    act_prev_ref[...] = activated(prev_ref[...], *before, tm > 0)

    @pl.when(tm >= 0)
    def _():
        for copy in weights:
            copy.wait()


def up_kernel(
    coef_ref,
    act_ref,
    act_prev_ref,
    above_ref,
    below_ref,
    w_first_ref,
    w_rest_ref,
    w_res_ref,
    hid_ref,
    sums_ref,
    w_res_out_ref,
    x_ref,
    acc_ref,
    sem,
):
    ahead = pltpu.make_async_copy(w_res_ref.at[0], w_res_out_ref, sem)
    ahead.start()
    tm, row, col = position()
    last_row = lax.axis_size("row") - 1
    scale, offset, scale_prev, offset_prev = (coef_ref[k : k + 1] for k in range(4))
    depth = scale.shape[-1]
    line = act_ref.shape[0] // 2
    span = line // SLOTS
    sent = above_ref.shape[0] // 2
    up, down = row > 0, row < last_row

    def active(piece, a, b, valid):
        return activated(piece[...], a, b, valid)

    take = narrow(ROWS * SLOTS)

    def place_span(block, part, at, a, b, valid):
        rows = [
            active(above_ref.at[part], a, b, valid & up),
            block[:line],
            block[line:],
            active(below_ref.at[part], a, b, valid & down),
        ]
        for f in range(span):
            frame = jnp.concatenate([r[f * SLOTS : (f + 1) * SLOTS] for r in rows], axis=0)
            x_ref[at + f] = jnp.dot(take, frame, preferred_element_type=F32).astype(BF16)

    place_span(act_prev_ref, slice(sent, 2 * sent), 0, scale_prev, offset_prev, tm > 0)
    place_span(act_ref, slice(0, sent), span, scale, offset, tm >= 0)
    acc_ref[0:2, SLOTS : SLOTS + ACROSS] = jnp.zeros((2, ACROSS, acc_ref.shape[-1]), F32)

    frames = 2 * span - 2
    size = frames * CELLS
    width = w_first_ref.shape[-1]
    up_bias = coef_ref[4:5, :width]
    for b in range(3):

        @pl.when(tm >= 0)
        def _():
            taps = w_first_ref if b == 0 else w_rest_ref.at[b - 1]
            x = jnp.concatenate([x_ref[a : a + frames].reshape(size, depth) for a in range(3)], axis=1)
            z = [
                jnp.dot(x, taps[:, e].reshape(3 * depth, width), preferred_element_type=F32) for e in range(3)
            ]
            even = pltpu.roll(z[0], 1, 0) + (z[1] + z[2])
            odd = (z[0] + z[1]) + pltpu.roll(z[2], size - 1, 0)
            for p in range(2):
                at = SLOTS + ACROSS * ((b == 0 and p == 0) - (b == 2 and p == 1))
                for q, u in ((0, even), (1, odd)):
                    k, rows = 2 * p + q, slice(at, at + size)
                    acc_ref[k, rows] = u if b == 0 else acc_ref[k, rows] + u

    total = jnp.zeros((1, width), F32)
    square = jnp.zeros((1, width), F32)
    line_of, c = by_twelve(lax.broadcasted_iota(jnp.int32, (span * CELLS, width), 0))
    r = line_of & (ROWS - 1)
    mine = (r >= 1) & (r <= 2) & (c >= 1) & (c <= 10)
    for k in range(4):
        hidden = (acc_ref[k, SLOTS : SLOTS + size] + up_bias).astype(BF16)
        for f in range(frames):
            hid_ref[f, k * CELLS : (k + 1) * CELLS] = hidden[f * CELLS : (f + 1) * CELLS]
        seen = jnp.where(mine, hidden[size - span * CELLS :].astype(F32), 0.0)
        total = total + jnp.sum(seen, axis=0, keepdims=True)
        square = square + jnp.sum(seen * seen, axis=0, keepdims=True)
    sums_ref[...] = jnp.broadcast_to(packed_sums(total, square), sums_ref.shape)
    ahead.wait()


def gather_matrix():
    m = np.zeros((3, 3, 20, 4, 2, 2, ROWS, ACROSS), np.float32)
    for b in range(3):
        for e in range(3):
            for y in range(4):
                for x in range(20):
                    v, u = y + b - 1, x + e - 1
                    m[b, e, x, y, v % 2, u % 2, v // 2 + 1, u // 2 + 1] = 1.0
    return m.reshape(720, 4 * CELLS)


def res_kernel(unit, parts_ref, gain_ref, bias_ref, b_ref, hid_ref, pick_ref, w_first_ref, w_ref, out_ref, g_ref, t_ref, wbuf, sems):
    copies = [pltpu.make_async_copy(w_ref.at[k + 1], wbuf.at[k], sems.at[k]) for k in range(2)]
    for copy in copies:
        copy.start()
    tm, row, col = position()
    last_row, last_col = lax.axis_size("row") - 1, lax.axis_size("col") - 1
    (scale, offset), (scale_prev, offset_prev) = affine(parts_ref[...], unit, gain_ref[...], bias_ref[...], tm)
    width = scale.shape[-1]
    line_of, slot = by_twelve(lax.broadcasted_iota(jnp.int32, (4 * CELLS, width), 0))
    parity, r = lax.shift_right_logical(line_of, 2), line_of & (ROWS - 1)
    y, x = 2 * (r - 1) + lax.shift_right_logical(parity, 1), 2 * (slot - 1) + (parity & 1)
    inside = ((y >= 0) | (row > 0)) & ((y < 4) | (row < last_row)) & ((x >= 0) | (col > 0)) & ((x < 20) | (col < last_col))
    n_now = out_ref.shape[0]
    n_prev = hid_ref.shape[0] - n_now
    area = 80
    for f in range(n_prev + n_now):
        a, b = (scale_prev, offset_prev) if f < n_prev else (scale, offset)
        valid = inside & (tm > 0) if f < n_prev else inside
        v = jnp.where(valid, silu(hid_ref[f].astype(F32) * a + b), 0.0)
        picked = jnp.dot(pick_ref[...], v.astype(BF16), preferred_element_type=F32).astype(BF16)
        for k in range(9):
            g_ref[f * area : (f + 1) * area, k * width : (k + 1) * width] = picked[k * area : (k + 1) * area]

    def part(a, w):
        slab = g_ref[a * area : (a + n_now) * area]
        return jnp.dot(slab, w.reshape(9 * width, width), preferred_element_type=F32)

    t_ref[...] = part(0, w_first_ref[...])

    @pl.when(tm >= 0)
    def _():
        for copy in copies:
            copy.wait()
        total = t_ref[...] + (part(1, wbuf[0]) + part(2, wbuf[1]))
        for f in range(n_now):
            hidden = jnp.dot(pick_ref[4 * area : 5 * area], hid_ref[n_prev + f], preferred_element_type=F32)
            decoded = total[f * area : (f + 1) * area] + b_ref[...] + hidden
            out_ref[f] = decoded.reshape(out_ref.shape[1:]).astype(BF16)


def shifted(value, spans, column):
    n_tm, n_col = lax.axis_size("tm"), lax.axis_size("col")
    route = [(t * n_col + c, (t + spans) % n_tm * n_col + column(c)) for t in range(n_tm) for c in range(n_col)]
    return lax.ppermute(value, ("tm", "col"), route)


def params(mib):
    return pltpu.CompilerParams(vmem_limit_bytes=mib * MIB)


def in_hbm(array):
    return pltpu.with_memory_space_constraint(array, pltpu.HBM)


VM = pl.BlockSpec(memory_space=pltpu.VMEM)
HBM = pl.BlockSpec(memory_space=pltpu.HBM)


def local(features, gain_low, bias_low, w_up, b_up, gain_high, bias_high, w_res, b_res):
    n_tm, n_row, n_col = (lax.axis_size(a) for a in EVERY)
    devices = n_tm * n_row * n_col
    frames, height, across, depth = features.shape
    width = w_up.shape[-1]
    low_unit = float(n_row * n_col * frames * height * across * (depth // GROUPS))
    high_unit = float(n_row * n_col * frames * 4 * height * across * (width // GROUPS))

    block = height * frames * SLOTS
    line = frames * SLOTS
    own, to_core, to_chip = pl.pallas_call(
        lay_out_kernel,
        out_shape=(
            jax.ShapeDtypeStruct((block, depth), BF16),
            jax.ShapeDtypeStruct((16, depth), BF16),
            jax.ShapeDtypeStruct((16, depth), BF16),
        ),
        in_specs=[VM],
        out_specs=(VM,) * 3,
        compiler_params=params(16),
        name="lay_out",
    )(features.transpose(0, 2, 1, 3))
    sums, w_first = pl.pallas_call(
        low_sums_kernel,
        out_shape=(jax.ShapeDtypeStruct((devices, LANES), F32), jax.ShapeDtypeStruct((3, 3, depth, width), BF16)),
        in_specs=[VM, HBM],
        out_specs=(HBM, VM),
        scratch_shapes=[pltpu.VMEM((devices, LANES), F32), pltpu.SemaphoreType.DMA((2,))],
        compiler_params=params(16),
        name="low_sums",
    )(own, in_hbm(w_up))
    prev_own = shifted(own, 1, lambda c: c)
    prev_core = shifted(to_core, 1, lambda c: c ^ 1)
    core = shifted(to_core, 0, lambda c: c ^ 1)
    prev_chip = shifted(to_chip, 1, lambda c: (c - 1 + 2 * (c % 2)) % n_col)
    chip = shifted(to_chip, 0, lambda c: (c - 1 + 2 * (c % 2)) % n_col)
    first = (chip, core, prev_chip, prev_core, prev_own)
    sums, first = lax.optimization_barrier((sums, first))
    chip, core, prev_chip, prev_core, prev_own = first
    low_parts = lax.all_to_all(sums, EVERY, 0, 0)
    gl, bl, bu = gain_low.reshape(1, -1), bias_low.reshape(1, -1), b_up.reshape(1, -1)
    gh, bh, br = gain_high.reshape(1, -1), bias_high.reshape(1, -1), b_res.reshape(1, -1)
    now, prev, up, down = pl.pallas_call(
        pack_kernel,
        out_shape=(jax.ShapeDtypeStruct((block, depth), BF16),) * 4,
        in_specs=[VM] * 6,
        out_specs=(VM,) * 4,
        compiler_params=params(16),
        name="pack",
    )(own, core, chip, prev_own, prev_core, prev_chip)
    above = lax.ppermute(down, "row", [(i, (i + 1) % n_row) for i in range(n_row)])
    below = lax.ppermute(up, "row", [(i, (i - 1) % n_row) for i in range(n_row)])
    coef, act, act_prev, w_rest = pl.pallas_call(
        functools.partial(fetch_kernel, low_unit),
        out_shape=(
            jax.ShapeDtypeStruct((8, depth), F32),
            jax.ShapeDtypeStruct((block, depth), BF16),
            jax.ShapeDtypeStruct((block, depth), BF16),
            jax.ShapeDtypeStruct((2, 3, 3, depth, width), BF16),
        ),
        in_specs=[VM] * 3 + [HBM] * 4,
        out_specs=(VM,) * 4,
        scratch_shapes=[
            pltpu.VMEM((1, depth), F32),
            pltpu.VMEM((1, depth), F32),
            pltpu.VMEM((1, width), F32),
            pltpu.SemaphoreType.DMA((3,)),
            pltpu.SemaphoreType.DMA((2,)),
        ],
        compiler_params=params(16),
        name="fetch",
    )(low_parts, now, prev, in_hbm(gl), in_hbm(bl), in_hbm(bu), in_hbm(w_up))
    hidden, high_sums, w_res_near = pl.pallas_call(
        up_kernel,
        out_shape=(
            jax.ShapeDtypeStruct((2 + frames, 4 * CELLS, width), BF16),
            jax.ShapeDtypeStruct((devices, LANES), F32),
            jax.ShapeDtypeStruct((3, 3, width, width), BF16),
        ),
        in_specs=[VM] * 7 + [HBM],
        out_specs=(VM,) * 3,
        scratch_shapes=[
            pltpu.VMEM((2 * frames, CELLS, depth), BF16),
            pltpu.VMEM((4, (2 + frames) * CELLS + 2 * SLOTS, width), F32),
            pltpu.SemaphoreType.DMA,
        ],
        compiler_params=params(20),
        name="up",
    )(coef, act, act_prev, above, below, w_first, w_rest, in_hbm(w_res))
    high_parts = lax.all_to_all(high_sums, EVERY, 0, 0)

    area = 4 * height * across
    decoded = pl.pallas_call(
        functools.partial(res_kernel, high_unit),
        out_shape=jax.ShapeDtypeStruct((frames, 2 * across, 2 * height, width), BF16),
        in_specs=[VM] * 7 + [HBM],
        out_specs=VM,
        scratch_shapes=[
            pltpu.VMEM(((2 + frames) * area, 9 * width), BF16),
            pltpu.VMEM((frames * area, width), F32),
            pltpu.VMEM((2, 3, 3, width, width), BF16),
            pltpu.SemaphoreType.DMA((2,)),
        ],
        compiler_params=params(24),
        name="res",
    )(high_parts, gh, bh, br, hidden, jnp.asarray(gather_matrix(), BF16), w_res_near, in_hbm(w_res))
    return decoded.transpose(0, 2, 1, 3)


def solution(mesh):
    in_specs = (P("tm", "row", "col", None), P(), P(), P(), P(), P(), P(), P(), P())
    out_specs = P("tm", "row", "col", None)
    return jax.shard_map(local, mesh=mesh, in_specs=in_specs, out_specs=out_specs, check_vma=False)
```
